32 devices in a mesh: ctx: 16 (over z, x, core), hd: 2 (over y).
Axes of the slice: x: 2, y: 2, z: 4, core: 2. Of those that a mesh axis runs over, the one named last changes fastest.
Arguments:
- query_rows: bfloat16 [4096, 4096], P('ctx', 'hd'), may hold values from -240 to 240
- key_rows: bfloat16 [4096, 1024], P('ctx', 'hd'), may hold values from -3.5 to 3.5
- value_rows: bfloat16 [4096, 1024], P('ctx', 'hd'), may hold values from -6 to 6
- doc_ids: int32 [64], P('ctx'), may hold values from 0 to 5, never falling along the last dimension, each value on 1 to 40 neighbouring positions
- out_weight: bfloat16 [4096, 4096], P('hd'), may hold values from -0.125 to 0.125
Outputs:
- attended: bfloat16 [4096, 4096], P('ctx', 'hd')
- projected: bfloat16 [4096, 4096], P('ctx', 'hd')
The draws below stay inside these ranges and needn't reach their ends.
Inputs may be any that keep to these rules, and one draw needn't show every extreme that they name: `doc_ids`: ids never fall along the stretch; each of the 6 documents spans 1 to 40 whole blocks, and one spans exactly 40.
All inputs are finite; a program needn't handle non-finite values.
Results may differ from the reference program's by a relative error of at most 0.019.
Values may be sent and summed in bfloat16 or wider, within the bound.
A program may use at most 64 MiB of HBM per device.

```python
import math
import jax
import jax.numpy as jnp
import numpy as np
from jax import lax

HEADS = 32
KVH = 8
HDIM = 128
D = 4096
BLOCK = 64
TOKENS = 4096
NBLK = 64
NDOCS = 6
MOSTB = 40


def key_values(key):
    sampled_values = jax.random.normal(jax.random.fold_in(key, 104), (TOKENS, KVH * HDIM), jnp.float32)
    return jnp.clip(sampled_values, -3.5, 3.5)


def draw_key_rows(key, part):
    sampled_values = key_values(key)
    return sampled_values.astype(jnp.bfloat16)


def draw_query_rows(key, part):
    key = jax.random.fold_in(key, 2)
    sampled_values = jnp.clip(jax.random.normal(key, (TOKENS, HEADS * HDIM), jnp.float32), -6.0, 6.0)
    return sampled_values.astype(jnp.bfloat16)


def spiked(drawn, key, source, target, blocks, factor):
    def block_of(dim):
        return (jnp.arange(drawn.shape[dim]) // (drawn.shape[dim] // blocks)).reshape((-1,) + (1,) * (drawn.ndim - 1 - dim))

    first = jax.random.permutation(key, blocks)[block_of(target)]
    other_side = (block_of(target) + blocks // 2) % blocks
    return jnp.where((block_of(source) == first) | (block_of(source) == other_side), factor * drawn, drawn)


def levels(stream_key, extent, split, least, top_value):
    loudness = 1.0
    for dim, parts in split:
        heights = jax.random.uniform(jax.random.fold_in(jax.random.fold_in(stream_key, 6), dim), (parts,), jnp.float32, least / len(split), top_value / len(split))
        loudness = loudness * jnp.repeat(jnp.exp(heights), extent[dim] // parts).reshape((-1,) + (1,) * (len(extent) - 1 - dim))
    return loudness


def split_up(count, total, most, lean):
    portions = [(1 << 20) // math.isqrt(rank ** lean) + 1 for rank in range(2, count + 1)]
    rest, given = total - most - (count - 1), [1] * (count - 1)
    while rest > 0:
        movable = [i for i in range(count - 1) if given[i] < most]
        mass, left = sum([portions[i] for i in movable]), rest
        for i in movable:
            addition = min(most - given[i], max(1, left * portions[i] // mass), rest)
            given[i] = given[i] + addition
            rest = rest - addition
    return np.array([most] + given)


def uneven(stream_key, amount, total, most, slope):
    if amount == 2:
        one = jax.random.randint(stream_key, (), max(1, total - most), min(most, total - 1) + 1)
        return jnp.stack([one, total - one])
    tallies = jnp.asarray(split_up(amount, total, most, slope), jnp.int32)
    pairs = (amount - 1) // 2
    source_of, receiver = tallies[1:1 + 2 * pairs:2], tallies[2:2 + 2 * pairs:2]
    room = jnp.minimum(source_of - 1, most - receiver)
    shifted = jax.random.randint(jax.random.fold_in(stream_key, 1), (pairs,), 0, 1 << 20) % (room + 1)
    tallies = tallies.at[1:1 + 2 * pairs:2].set(source_of - shifted).at[2:2 + 2 * pairs:2].set(receiver + shifted)
    return tallies[jax.random.permutation(jax.random.fold_in(stream_key, 2), amount)]


def normal_values(own_key, extent, deviation, most, split=(), kind=jnp.bfloat16):
    values = deviation * jax.random.normal(own_key, extent, jnp.float32)
    if split:
        values = values * levels(own_key, extent, split, -0.22, 0.18)
    return jnp.clip(values, -most, most).astype(kind)


def noise_with(key, extent, deviation, most, cuts, heavy, held_as=jnp.bfloat16):
    values = deviation * jax.random.normal(key, extent, jnp.float32)
    if cuts:
        values = values * levels(key, extent, cuts, -0.22, 0.18)
    return jnp.clip(spiked(values, jax.random.fold_in(key, 3), *heavy), -most, most).astype(held_as)


def setup_inputs(seed: int = 0) -> dict:
    key_of = jax.random.split(jax.random.key(seed), 6)
    query_rows = draw_query_rows(jax.random.fold_in(key_of[5], 71), 0)
    key_rows = draw_key_rows(jax.random.fold_in(key_of[5], 71), 0)
    value_rows = normal_values(key_of[2], (TOKENS, KVH * HDIM), 1.0, 6.0, ((0, 16), (1, 2)))
    doc_ids = jnp.searchsorted(jnp.cumsum(uneven(key_of[3], NDOCS, NBLK, MOSTB, 2)), jnp.arange(NBLK), side="right").astype(jnp.int32)
    out_weight = noise_with(key_of[4], (HEADS * HDIM, D), (HEADS * HDIM) ** -0.5, 0.125, ((0, 2),), (0, 1, 2, 2.0))
    return dict(query_rows=query_rows, key_rows=key_rows, value_rows=value_rows, doc_ids=doc_ids, out_weight=out_weight)


NEG_BIG = -1.0e30


def attention_reference(query_rows, key_rows, value_rows, doc_ids):
    group_size = HEADS // KVH
    query_block = min(TOKENS, 256)
    block_total = TOKENS // query_block
    score_scale = 1.0 / (HDIM ** 0.5)
    token_docs = jnp.repeat(doc_ids, BLOCK)
    key_pos = jnp.arange(TOKENS, dtype=jnp.int32)
    key_heads = key_rows.astype(jnp.float32).reshape(TOKENS, KVH, HDIM).transpose(1, 0, 2)
    value_heads = value_rows.astype(jnp.float32).reshape(TOKENS, KVH, HDIM).transpose(1, 0, 2)
    query_all = query_rows.astype(jnp.float32).reshape(TOKENS, KVH, group_size, HDIM)

    def one_block(block_index):
        leading_row = (block_index * query_block).astype(jnp.int32)
        query_part = lax.dynamic_slice_in_dim(query_all, leading_row, query_block, 0)
        query_pos = leading_row + jnp.arange(query_block, dtype=jnp.int32)
        query_doc = lax.dynamic_slice_in_dim(token_docs, leading_row, query_block, 0)
        visible = (key_pos[None, :] <= query_pos[:, None]) & (token_docs[None, :] == query_doc[:, None])

        def one_head(head_inputs):
            head_queries, head_keys, head_values = head_inputs
            scores = jnp.einsum("tgd,sd->gts", head_queries, head_keys) * score_scale
            scores = jnp.where(visible[None], scores, NEG_BIG)
            row_max = jnp.max(scores, axis=-1, keepdims=True)
            weights = jnp.where(visible[None], jnp.exp(scores - row_max), 0.0)
            row_sum = jnp.sum(weights, axis=-1)
            rounded = lax.optimization_barrier(weights.astype(jnp.bfloat16)).astype(jnp.float32)
            summed = jnp.einsum("gts,sd->tgd", rounded, head_values)
            return summed / row_sum.T[:, :, None]

        return lax.map(one_head, (query_part.transpose(1, 0, 2, 3), key_heads, value_heads))

    blocks_out = lax.map(one_block, jnp.arange(block_total, dtype=jnp.int32))
    return blocks_out.transpose(0, 2, 1, 3, 4).reshape(TOKENS, HEADS * HDIM).astype(jnp.bfloat16)


def reference(query_rows, key_rows, value_rows, doc_ids, out_weight):
    attended = attention_reference(query_rows, key_rows, value_rows, doc_ids)
    projected = jnp.dot(attended, out_weight, preferred_element_type=jnp.float32).astype(jnp.bfloat16)
    return attended, projected
```

```python
from functools import partial
import math

import jax
import jax.numpy as jnp
from jax import lax
from jax.experimental import pallas as pl
from jax.experimental.pallas import tpu as pltpu
from jax.sharding import PartitionSpec as P

HDIM = 128
BLOCK = 64


NEG_BIG = -1e30


def attend_part(
    softmax_state, shard_part, leading_row, query_heads, query_pos, query_doc, score_scale
):
    key_part, value_part, doc_part = shard_part
    row_count = key_part.shape[0]
    block_len = 256
    kv_local = query_heads.shape[1]
    key_blocks = key_part.reshape(row_count // block_len, block_len, kv_local, HDIM)
    value_blocks = value_part.reshape(row_count // block_len, block_len, kv_local, HDIM)
    doc_blocks = doc_part.reshape(row_count // block_len, block_len)

    def one_block(block_index, running):
        block_keys = key_blocks[block_index]
        block_values = value_blocks[block_index]
        key_pos = block_index * block_len + jnp.arange(block_len, dtype=jnp.int32)
        visible = (key_pos[None, :] <= query_pos[:, None]) & (key_pos[None, :] >= 0)
        visible = visible & (doc_blocks[block_index][None, :] == query_doc[:, None])

        def compute(inner_state):
            old_max, old_sum, old_weighted = inner_state
            scores = (
                jnp.einsum(
                    "tkgd,skd->kgts", query_heads, block_keys, preferred_element_type=jnp.float32
                )
                * score_scale
            )
            scores = jnp.where(visible[None, None], scores, NEG_BIG)
            new_max = jnp.maximum(old_max, jnp.max(scores, axis=-1))
            factor = jnp.exp(old_max - new_max)
            weights = jnp.where(visible[None, None], jnp.exp(scores - new_max[..., None]), 0.0)
            new_sum = old_sum * factor + jnp.sum(weights, axis=-1)
            update = jnp.einsum(
                "kgts,skd->kgtd",
                weights.astype(jnp.bfloat16),
                block_values,
                preferred_element_type=jnp.float32,
            )
            return (new_max, new_sum, old_weighted * factor[..., None] + update)

        return lax.cond(jnp.any(visible), compute, lambda inner_state: inner_state, running)

    return lax.fori_loop(0, row_count // block_len, one_block, softmax_state)


def attention_part(query_rows, key_rows, value_rows, doc_ids):
    tokens_here = query_rows.shape[0]
    kv_local = key_rows.shape[1] // HDIM
    group_size = query_rows.shape[1] // key_rows.shape[1]
    position = lax.axis_index("ctx")
    query_heads = query_rows.reshape(tokens_here, kv_local, group_size, HDIM)
    query_pos = position * tokens_here + jnp.arange(tokens_here, dtype=jnp.int32)
    token_docs = jnp.repeat(doc_ids, BLOCK)
    fold_part = partial(
        attend_part,
        query_heads=query_heads,
        query_pos=query_pos,
        query_doc=token_docs,
        score_scale=1.0 / math.sqrt(HDIM),
    )
    start_state = (
        jnp.full((kv_local, group_size, tokens_here), NEG_BIG, jnp.float32),
        jnp.zeros((kv_local, group_size, tokens_here), jnp.float32),
        jnp.zeros((kv_local, group_size, tokens_here, HDIM), jnp.float32),
    )
    softmax_state = fold_part(
        start_state,
        (
            lax.all_gather(key_rows, "ctx", axis=0, tiled=True),
            lax.all_gather(value_rows, "ctx", axis=0, tiled=True),
            lax.all_gather(token_docs, "ctx", axis=0, tiled=True),
        ),
        jnp.int32(0),
    )
    final_max, final_sum, final_weighted = softmax_state
    attended = final_weighted / final_sum[..., None]
    return (
        attended.transpose(2, 0, 1, 3)
        .reshape(tokens_here, kv_local * group_size * HDIM)
        .astype(jnp.bfloat16)
    )


def per_device(query_rows, key_rows, value_rows, doc_ids, out_weight):
    attended = attention_part(query_rows, key_rows, value_rows, doc_ids)
    partial_proj = jnp.dot(attended, out_weight, preferred_element_type=jnp.float32)
    projected = lax.psum_scatter(
        partial_proj.astype(jnp.bfloat16), "hd", scatter_dimension=1, tiled=True
    )
    return (attended, projected)

NEG_MASK = -1e30
LOG2E = 1.4426950408889634
MESH = pl.DeviceIdType.MESH


def fused_kernel(
    levels, reach, q_ref, k_ref, v_ref, doc_ref, w_ref, att_ref, proj_ref,
    buf, qa, acc, mrow, lrow, wbuf, psend, pown, precv,
    send_sem, recv_sem, w_sem, ysend_sem, yrecv_sem,
):
    rows = q_ref.shape[0]
    kv_local = k_ref.shape[1] // HDIM
    group = q_ref.shape[1] // k_ref.shape[1]
    scale = LOG2E / math.sqrt(HDIM)
    v_at = rows + 16
    me = lax.axis_index("ctx")
    half = lax.axis_index("hd")
    z, x, c = lax.div(me, 4), lax.rem(lax.div(me, 2), 2), lax.rem(me, 2)
    up, across, sibling = me + 4, 4 * z + 2 * (1 - x) + c, 4 * z + 2 * x + (1 - c)
    across_chip = 4 * z + 2 * (1 - x)

    w_copy = pltpu.make_async_copy(w_ref, wbuf, w_sem)
    w_copy.start()

    barrier = pltpu.get_barrier_semaphore()
    pl.semaphore_signal(barrier, inc=1, device_id={"ctx": across}, device_id_type=MESH)
    pl.semaphore_signal(barrier, inc=1, device_id={"ctx": sibling}, device_id_type=MESH)
    pl.semaphore_signal(barrier, inc=1, device_id={"hd": 1 - half}, device_id_type=MESH)

    @pl.when(z + 1 < levels)
    def _():
        pl.semaphore_signal(barrier, inc=1, device_id={"ctx": up}, device_id_type=MESH)

    @pl.when(z > 0)
    def _():
        pl.semaphore_signal(barrier, inc=1, device_id={"ctx": me - 4}, device_id_type=MESH)

    buf[me, 0:rows, :] = k_ref[...]
    buf[me, rows:v_at, :] = doc_ref[...]
    buf[me, v_at:, :] = v_ref[...]

    pl.semaphore_wait(
        barrier, 3 + jnp.where(z + 1 < levels, 1, 0) + jnp.where(z > 0, 1, 0)
    )

    parts = ((0, v_at), (v_at, rows))

    def copy(src, part, direction, target):
        ref = buf.at[src, pl.ds(parts[part][0], parts[part][1])]
        return pltpu.make_async_remote_copy(
            src_ref=ref, dst_ref=ref,
            send_sem=send_sem.at[direction, src, part],
            recv_sem=recv_sem.at[src, part],
            device_id={"ctx": target}, device_id_type=MESH,
        )

    def sends(src, column):
        return (
            (0, up, column & (z + 1 < levels) & (4 * (z + 1) - src <= reach)),
            (1, across, column & (src < across_chip) & (across_chip - src <= reach)),
            (2, sibling, (sibling > src) & (sibling - src <= reach)),
        )

    def forward(src, column, part):
        for direction, target, needed in sends(src, column):
            @pl.when(needed)
            def _():
                copy(src, part, direction, target).start()

    def drain(src, column):
        for direction, target, needed in sends(src, column):
            @pl.when(needed)
            def _():
                for part in range(2):
                    copy(src, part, direction, target).wait_send()

    always = me >= 0
    for part in range(2):
        forward(me, always, part)

    lane = lax.broadcasted_iota(jnp.int32, (1, rows), 1)
    docs = doc_ref[...].astype(jnp.float32)
    query_doc = jnp.zeros((1, rows), jnp.float32)
    for b in range(rows // BLOCK):
        inside = (lane >= b * BLOCK) & (lane < (b + 1) * BLOCK)
        query_doc = jnp.where(inside, docs[b : b + 1, 0:rows], query_doc)
    ids = lax.broadcasted_iota(jnp.int32, (HDIM, rows), 0).astype(jnp.float32)
    onehot = jnp.where(ids == query_doc, 1.0, 0.0).astype(jnp.bfloat16)
    for kv in range(kv_local):
        for g in range(group):
            head = (kv * group + g) * HDIM
            cols = slice(g * rows, (g + 1) * rows)
            qa[kv, 0:HDIM, cols] = q_ref[:, head : head + HDIM].T
            qa[kv, HDIM:, cols] = onehot

    def attend(src, diagonal):
        shard_docs = buf[src, rows:v_at, 0:HDIM].astype(jnp.float32)
        doc_lane = lax.broadcasted_iota(jnp.int32, (BLOCK, HDIM), 1).astype(jnp.float32)
        key_mask = jnp.concatenate(
            [
                jnp.where(doc_lane == shard_docs[b : b + 1, :], 0.0, NEG_MASK)
                for b in range(rows // BLOCK)
            ],
            axis=0,
        ).astype(jnp.bfloat16)

        @pl.loop(0, kv_local)
        def _(kv):
            at = pl.ds(pl.multiple_of(kv * HDIM, HDIM), HDIM)
            keys = jnp.concatenate([buf[src, 0:rows, at], key_mask], axis=1)
            values = buf[src, v_at:, at]
            for g in range(group):
                cols = slice(g * rows, (g + 1) * rows)
                scores = jnp.dot(keys, qa[kv, :, cols], preferred_element_type=jnp.float32)
                if diagonal:
                    key_pos = lax.broadcasted_iota(jnp.int32, scores.shape, 0)
                    query_pos = lax.broadcasted_iota(jnp.int32, scores.shape, 1)
                    scores = jnp.where(key_pos <= query_pos, scores, NEG_MASK)
                top = jnp.max(scores, axis=0, keepdims=True)
                if not diagonal:
                    old = mrow[kv, 0:1, cols]
                    top = jnp.maximum(top, old)
                    factor = jnp.exp2((old - top) * scale)
                weights = jnp.exp2((scores - top) * scale)
                total = jnp.sum(weights, axis=0, keepdims=True)
                update = lax.dot_general(
                    values, weights.astype(jnp.bfloat16), (((0,), (0,)), ((), ())),
                    preferred_element_type=jnp.float32,
                )
                if not diagonal:
                    total = total + lrow[kv, 0:1, cols] * factor
                    update = update + acc[kv, :, cols] * factor
                mrow[kv, 0:1, cols] = top
                lrow[kv, 0:1, cols] = total
                acc[kv, :, cols] = update

    attend(me, True)

    def event(step):
        kind = lax.rem(step, 4)
        back = lax.div(step, 4) - jnp.where(kind >= 2, 1, 0)
        src_z = z - back
        src_x = jnp.where(kind >= 2, 1 - x, x)
        src_c = jnp.where(lax.rem(kind, 2) == 1, 1 - c, c)
        src = 4 * src_z + 2 * src_x + src_c
        near = (src < me) & (me - src <= reach)
        chip = 4 * z + 2 * x
        by_level = (kind == 0) & (back >= 1) & (4 * z - src <= reach)
        by_across = (kind == 2) & (src < chip) & (chip - src <= reach)
        by_sibling = (lax.rem(kind, 2) == 1) & near
        held = (back >= 0) & (src_z >= 0) & (by_level | by_across | by_sibling)
        return src, kind, held, held & near

    @pl.loop(0, 4 * (levels + 1))
    def _(step):
        src, kind, held, near = event(step)

        @pl.when(held)
        def _():
            for part in range(2):
                copy(src, part, 0, sibling).wait_recv()

                @pl.when(lax.rem(kind, 2) == 0)
                def _():
                    forward(src, kind == 0, part)

        @pl.when(near)
        def _():
            attend(src, False)

    @pl.loop(0, kv_local)
    def _(kv):
        for g in range(group):
            cols = slice(g * rows, (g + 1) * rows)
            head = acc[kv, :, cols] / lrow[kv, 0:1, cols]
            at = pl.ds(pl.multiple_of((kv * group + g) * HDIM, HDIM), HDIM)
            att_ref[:, at] = head.T.astype(jnp.bfloat16)

    w_copy.wait()
    chunks, _, width = psend.shape

    def exchange(n):
        return pltpu.make_async_remote_copy(
            src_ref=psend.at[n], dst_ref=precv.at[n],
            send_sem=ysend_sem.at[n], recv_sem=yrecv_sem.at[n],
            device_id={"hd": 1 - half}, device_id_type=MESH,
        )

    def project(first, n):
        at = pl.ds(pl.multiple_of((first * chunks + n) * width, width), width)
        return jnp.dot(att_ref[...], wbuf[:, at], preferred_element_type=jnp.float32)

    @pl.loop(0, chunks)
    def _(n):
        psend[n] = project(1 - half, n).astype(jnp.bfloat16)
        exchange(n).start()

    @pl.loop(0, chunks)
    def _(n):
        pown[n] = project(half, n)

    for n in range(chunks):
        exchange(n).wait_recv()
        proj_ref[:, n * width : (n + 1) * width] = (
            pown[n] + precv[n].astype(jnp.float32)
        ).astype(jnp.bfloat16)

    for n in range(chunks):
        exchange(n).wait_send()
    drain(me, always)

    @pl.loop(0, 4 * (levels + 1))
    def _(step):
        src, kind, held, _near = event(step)

        @pl.when(held & (lax.rem(kind, 2) == 0))
        def _():
            drain(src, kind == 0)


def fused_device(ctx_size, query_rows, key_rows, value_rows, doc_ids, out_weight):
    rows, q_cols = query_rows.shape
    kv_cols = key_rows.shape[1]
    kv_local = kv_cols // HDIM
    group = q_cols // kv_cols
    shard_blocks = rows // BLOCK
    reach = -(-(ctx_size * shard_blocks * 5 // 8 - 1) // shard_blocks)
    width = 512
    out_cols = out_weight.shape[1] // 2
    chunks = out_cols // width
    doc_tile = jnp.zeros((16, kv_cols), jnp.bfloat16).at[0:shard_blocks].set(
        jnp.broadcast_to(doc_ids.astype(jnp.bfloat16)[:, None], (shard_blocks, kv_cols))
    )
    vmem = pl.BlockSpec(memory_space=pltpu.VMEM)
    return pl.pallas_call(
        partial(fused_kernel, ctx_size // 4, reach),
        out_shape=(
            jax.ShapeDtypeStruct((rows, q_cols), jnp.bfloat16),
            jax.ShapeDtypeStruct((rows, out_cols), jnp.bfloat16),
        ),
        in_specs=[vmem] * 4 + [pl.BlockSpec(memory_space=pl.ANY)],
        out_specs=(vmem, vmem),
        scratch_shapes=[
            pltpu.VMEM((ctx_size, 2 * rows + 16, kv_cols), jnp.bfloat16),
            pltpu.VMEM((kv_local, 2 * HDIM, group * rows), jnp.bfloat16),
            pltpu.VMEM((kv_local, HDIM, group * rows), jnp.float32),
            pltpu.VMEM((kv_local, 8, group * rows), jnp.float32),
            pltpu.VMEM((kv_local, 8, group * rows), jnp.float32),
            pltpu.VMEM(out_weight.shape, jnp.bfloat16),
            pltpu.VMEM((chunks, rows, width), jnp.bfloat16),
            pltpu.VMEM((chunks, rows, width), jnp.float32),
            pltpu.VMEM((chunks, rows, width), jnp.bfloat16),
            pltpu.SemaphoreType.DMA((3, ctx_size, 2)),
            pltpu.SemaphoreType.DMA((ctx_size, 2)),
            pltpu.SemaphoreType.DMA,
            pltpu.SemaphoreType.DMA((chunks,)),
            pltpu.SemaphoreType.DMA((chunks,)),
        ],
        compiler_params=pltpu.CompilerParams(
            collective_id=0, has_side_effects=True, vmem_limit_bytes=52 * 1024 * 1024
        ),
    )(query_rows, key_rows, value_rows, doc_tile, out_weight)


def solution(mesh):
    in_specs = (P("ctx", "hd"), P("ctx", "hd"), P("ctx", "hd"), P("ctx"), P("hd", None))
    out_specs = (P("ctx", "hd"), P("ctx", "hd"))
    body = per_device
    if mesh.shape["ctx"] == 16 and mesh.shape["hd"] == 2:
        body = partial(fused_device, mesh.shape["ctx"])
    return jax.shard_map(
        body, mesh=mesh, in_specs=in_specs, out_specs=out_specs, check_vma=False
    )
```

```python
from functools import partial
import math

import jax
import jax.numpy as jnp
from jax import lax
from jax.experimental import pallas as pl
from jax.experimental.pallas import tpu as pltpu
from jax.sharding import PartitionSpec as P

HDIM = 128
BLOCK = 64


NEG_BIG = -1e30


def attend_part(
    softmax_state, shard_part, leading_row, query_heads, query_pos, query_doc, score_scale
):
    key_part, value_part, doc_part = shard_part
    row_count = key_part.shape[0]
    block_len = 256
    kv_local = query_heads.shape[1]
    key_blocks = key_part.reshape(row_count // block_len, block_len, kv_local, HDIM)
    value_blocks = value_part.reshape(row_count // block_len, block_len, kv_local, HDIM)
    doc_blocks = doc_part.reshape(row_count // block_len, block_len)

    def one_block(block_index, running):
        block_keys = key_blocks[block_index]
        block_values = value_blocks[block_index]
        key_pos = block_index * block_len + jnp.arange(block_len, dtype=jnp.int32)
        visible = (key_pos[None, :] <= query_pos[:, None]) & (key_pos[None, :] >= 0)
        visible = visible & (doc_blocks[block_index][None, :] == query_doc[:, None])

        def compute(inner_state):
            old_max, old_sum, old_weighted = inner_state
            scores = (
                jnp.einsum(
                    "tkgd,skd->kgts", query_heads, block_keys, preferred_element_type=jnp.float32
                )
                * score_scale
            )
            scores = jnp.where(visible[None, None], scores, NEG_BIG)
            new_max = jnp.maximum(old_max, jnp.max(scores, axis=-1))
            factor = jnp.exp(old_max - new_max)
            weights = jnp.where(visible[None, None], jnp.exp(scores - new_max[..., None]), 0.0)
            new_sum = old_sum * factor + jnp.sum(weights, axis=-1)
            update = jnp.einsum(
                "kgts,skd->kgtd",
                weights.astype(jnp.bfloat16),
                block_values,
                preferred_element_type=jnp.float32,
            )
            return (new_max, new_sum, old_weighted * factor[..., None] + update)

        return lax.cond(jnp.any(visible), compute, lambda inner_state: inner_state, running)

    return lax.fori_loop(0, row_count // block_len, one_block, softmax_state)


def attention_part(query_rows, key_rows, value_rows, doc_ids):
    tokens_here = query_rows.shape[0]
    kv_local = key_rows.shape[1] // HDIM
    group_size = query_rows.shape[1] // key_rows.shape[1]
    position = lax.axis_index("ctx")
    query_heads = query_rows.reshape(tokens_here, kv_local, group_size, HDIM)
    query_pos = position * tokens_here + jnp.arange(tokens_here, dtype=jnp.int32)
    token_docs = jnp.repeat(doc_ids, BLOCK)
    fold_part = partial(
        attend_part,
        query_heads=query_heads,
        query_pos=query_pos,
        query_doc=token_docs,
        score_scale=1.0 / math.sqrt(HDIM),
    )
    start_state = (
        jnp.full((kv_local, group_size, tokens_here), NEG_BIG, jnp.float32),
        jnp.zeros((kv_local, group_size, tokens_here), jnp.float32),
        jnp.zeros((kv_local, group_size, tokens_here, HDIM), jnp.float32),
    )
    softmax_state = fold_part(
        start_state,
        (
            lax.all_gather(key_rows, "ctx", axis=0, tiled=True),
            lax.all_gather(value_rows, "ctx", axis=0, tiled=True),
            lax.all_gather(token_docs, "ctx", axis=0, tiled=True),
        ),
        jnp.int32(0),
    )
    final_max, final_sum, final_weighted = softmax_state
    attended = final_weighted / final_sum[..., None]
    return (
        attended.transpose(2, 0, 1, 3)
        .reshape(tokens_here, kv_local * group_size * HDIM)
        .astype(jnp.bfloat16)
    )


def per_device(query_rows, key_rows, value_rows, doc_ids, out_weight):
    attended = attention_part(query_rows, key_rows, value_rows, doc_ids)
    partial_proj = jnp.dot(attended, out_weight, preferred_element_type=jnp.float32)
    projected = lax.psum_scatter(
        partial_proj.astype(jnp.bfloat16), "hd", scatter_dimension=1, tiled=True
    )
    return (attended, projected)

NEG_MASK = -1e30
LOG2E = 1.4426950408889634
MESH = pl.DeviceIdType.MESH


def fused_kernel(
    levels, reach, q_ref, k_ref, v_ref, doc_ref, w_ref, att_ref, proj_ref,
    buf, qa, acc, mrow, lrow, wbuf, psend, pown, precv,
    send_sem, recv_sem, w_sem, ysend_sem, yrecv_sem,
):
    rows = q_ref.shape[0]
    kv_local = k_ref.shape[1] // HDIM
    group = q_ref.shape[1] // k_ref.shape[1]
    scale = LOG2E / math.sqrt(HDIM)
    v_at = rows + 16
    me = lax.axis_index("ctx")
    half = lax.axis_index("hd")
    z, x, c = lax.div(me, 4), lax.rem(lax.div(me, 2), 2), lax.rem(me, 2)
    up, across, sibling = me + 4, 4 * z + 2 * (1 - x) + c, 4 * z + 2 * x + (1 - c)
    across_chip = 4 * z + 2 * (1 - x)

    w_copy = pltpu.make_async_copy(w_ref, wbuf, w_sem)
    w_copy.start()

    barrier = pltpu.get_barrier_semaphore()
    pl.semaphore_signal(barrier, inc=1, device_id={"ctx": across}, device_id_type=MESH)
    pl.semaphore_signal(barrier, inc=1, device_id={"ctx": sibling}, device_id_type=MESH)
    pl.semaphore_signal(barrier, inc=1, device_id={"hd": 1 - half}, device_id_type=MESH)

    @pl.when(z + 1 < levels)
    def _():
        pl.semaphore_signal(barrier, inc=1, device_id={"ctx": up}, device_id_type=MESH)

    @pl.when(z > 0)
    def _():
        pl.semaphore_signal(barrier, inc=1, device_id={"ctx": me - 4}, device_id_type=MESH)

    buf[me, 0:rows, :] = k_ref[...]
    buf[me, rows:v_at, :] = doc_ref[...]
    buf[me, v_at:, :] = v_ref[...]

    pl.semaphore_wait(
        barrier, 3 + jnp.where(z + 1 < levels, 1, 0) + jnp.where(z > 0, 1, 0)
    )

    middle = rows // 2
    parts = (
        (0, middle), (middle, v_at - middle), (v_at, middle), (v_at + middle, rows - middle)
    )

    def copy(src, part, direction, target):
        ref = buf.at[src, pl.ds(parts[part][0], parts[part][1])]
        return pltpu.make_async_remote_copy(
            src_ref=ref, dst_ref=ref,
            send_sem=send_sem.at[direction, src, part],
            recv_sem=recv_sem.at[src, part],
            device_id={"ctx": target}, device_id_type=MESH,
        )

    def sends(src, column):
        return (
            (0, up, column & (z + 1 < levels) & (4 * (z + 1) - src <= reach)),
            (1, across, column & (src < across_chip) & (across_chip - src <= reach)),
            (2, sibling, (sibling > src) & (sibling - src <= reach)),
        )

    def forward(src, column, part):
        for direction, target, needed in sends(src, column):
            @pl.when(needed)
            def _():
                copy(src, part, direction, target).start()

    def drain(src, column):
        for direction, target, needed in sends(src, column):
            @pl.when(needed)
            def _():
                for part in range(len(parts)):
                    copy(src, part, direction, target).wait_send()

    always = me >= 0
    for part in range(len(parts)):
        forward(me, always, part)

    lane = lax.broadcasted_iota(jnp.int32, (1, rows), 1)
    docs = doc_ref[...].astype(jnp.float32)
    query_doc = jnp.zeros((1, rows), jnp.float32)
    for b in range(rows // BLOCK):
        inside = (lane >= b * BLOCK) & (lane < (b + 1) * BLOCK)
        query_doc = jnp.where(inside, docs[b : b + 1, 0:rows], query_doc)
    ids = lax.broadcasted_iota(jnp.int32, (HDIM, rows), 0).astype(jnp.float32)
    onehot = jnp.where(ids == query_doc, 1.0, 0.0).astype(jnp.bfloat16)
    for kv in range(kv_local):
        for g in range(group):
            head = (kv * group + g) * HDIM
            cols = slice(g * rows, (g + 1) * rows)
            qa[kv, 0:HDIM, cols] = q_ref[:, head : head + HDIM].T
            qa[kv, HDIM:, cols] = onehot

    def attend(src, diagonal):
        shard_docs = buf[src, rows:v_at, 0:HDIM].astype(jnp.float32)
        doc_lane = lax.broadcasted_iota(jnp.int32, (BLOCK, HDIM), 1).astype(jnp.float32)
        key_mask = jnp.concatenate(
            [
                jnp.where(doc_lane == shard_docs[b : b + 1, :], 0.0, NEG_MASK)
                for b in range(rows // BLOCK)
            ],
            axis=0,
        ).astype(jnp.bfloat16)

        heads = [(kv, g) for kv in range(kv_local) for g in range(group)]
        keys_of, values_of = {}, {}

        def scores_of(kv, g):
            if kv not in keys_of:
                at = slice(kv * HDIM, (kv + 1) * HDIM)
                keys_of[kv] = jnp.concatenate([buf[src, 0:rows, at], key_mask], axis=1)
                values_of[kv] = buf[src, v_at:, at].T
            scores = jnp.dot(
                keys_of[kv],
                qa[kv, :, g * rows : (g + 1) * rows],
                preferred_element_type=jnp.float32,
            )
            if diagonal:
                key_pos = lax.broadcasted_iota(jnp.int32, scores.shape, 0)
                query_pos = lax.broadcasted_iota(jnp.int32, scores.shape, 1)
                scores = jnp.where(key_pos <= query_pos, scores, NEG_MASK)
            return scores

        ahead = 2
        ready = [scores_of(*head) for head in heads[:ahead]]
        for index, (kv, g) in enumerate(heads):
            cols = slice(g * rows, (g + 1) * rows)
            scores = ready.pop(0)
            if index + ahead < len(heads):
                ready.append(scores_of(*heads[index + ahead]))
            top = jnp.max(scores, axis=0, keepdims=True)
            if not diagonal:
                old = mrow[kv, 0:1, cols]
                top = jnp.maximum(top, old)
                factor = jnp.exp2((old - top) * scale)
            weights = jnp.exp2((scores - top) * scale)
            total = jnp.sum(weights, axis=0, keepdims=True)
            update = jnp.dot(
                values_of[kv], weights.astype(jnp.bfloat16), preferred_element_type=jnp.float32
            )
            if not diagonal:
                total = total + lrow[kv, 0:1, cols] * factor
                update = update + acc[kv, :, cols] * factor
            mrow[kv, 0:1, cols] = top
            lrow[kv, 0:1, cols] = total
            acc[kv, :, cols] = update

    attend(me, True)

    def event(step):
        kind = lax.rem(step, 4)
        back = lax.div(step, 4) - jnp.where(kind >= 2, 1, 0)
        src_z = z - back
        src_x = jnp.where(kind >= 2, 1 - x, x)
        src_c = jnp.where(lax.rem(kind, 2) == 1, 1 - c, c)
        src = 4 * src_z + 2 * src_x + src_c
        near = (src < me) & (me - src <= reach)
        chip = 4 * z + 2 * x
        by_level = (kind == 0) & (back >= 1) & (4 * z - src <= reach)
        by_across = (kind == 2) & (src < chip) & (chip - src <= reach)
        by_sibling = (lax.rem(kind, 2) == 1) & near
        held = (back >= 0) & (src_z >= 0) & (by_level | by_across | by_sibling)
        return src, kind, held, held & near

    @pl.loop(0, 4 * (levels + 1))
    def _(step):
        src, kind, held, near = event(step)

        @pl.when(held)
        def _():
            for part in range(len(parts)):
                copy(src, part, 0, sibling).wait_recv()

                @pl.when(lax.rem(kind, 2) == 0)
                def _():
                    forward(src, kind == 0, part)

        @pl.when(near)
        def _():
            attend(src, False)

    @pl.loop(0, kv_local)
    def _(kv):
        for g in range(group):
            cols = slice(g * rows, (g + 1) * rows)
            head = acc[kv, :, cols] / lrow[kv, 0:1, cols]
            at = pl.ds(pl.multiple_of((kv * group + g) * HDIM, HDIM), HDIM)
            att_ref[:, at] = head.T.astype(jnp.bfloat16)

    w_copy.wait()
    chunks, _, width = psend.shape

    def exchange(n):
        return pltpu.make_async_remote_copy(
            src_ref=psend.at[n], dst_ref=precv.at[n],
            send_sem=ysend_sem.at[n], recv_sem=yrecv_sem.at[n],
            device_id={"hd": 1 - half}, device_id_type=MESH,
        )

    def project(first, n):
        at = pl.ds(pl.multiple_of((first * chunks + n) * width, width), width)
        return jnp.dot(att_ref[...], wbuf[:, at], preferred_element_type=jnp.float32)

    @pl.loop(0, chunks)
    def _(n):
        psend[n] = project(1 - half, n).astype(jnp.bfloat16)
        exchange(n).start()

    @pl.loop(0, chunks)
    def _(n):
        pown[n] = project(half, n)

    for n in range(chunks):
        exchange(n).wait_recv()
        proj_ref[:, n * width : (n + 1) * width] = (
            pown[n] + precv[n].astype(jnp.float32)
        ).astype(jnp.bfloat16)

    for n in range(chunks):
        exchange(n).wait_send()
    drain(me, always)

    @pl.loop(0, 4 * (levels + 1))
    def _(step):
        src, kind, held, _near = event(step)

        @pl.when(held & (lax.rem(kind, 2) == 0))
        def _():
            drain(src, kind == 0)


def fused_device(ctx_size, query_rows, key_rows, value_rows, doc_ids, out_weight):
    rows, q_cols = query_rows.shape
    kv_cols = key_rows.shape[1]
    kv_local = kv_cols // HDIM
    group = q_cols // kv_cols
    shard_blocks = rows // BLOCK
    reach = -(-(ctx_size * shard_blocks * 5 // 8 - 1) // shard_blocks)
    width = 512
    out_cols = out_weight.shape[1] // 2
    chunks = out_cols // width
    doc_tile = jnp.zeros((16, kv_cols), jnp.bfloat16).at[0:shard_blocks].set(
        jnp.broadcast_to(doc_ids.astype(jnp.bfloat16)[:, None], (shard_blocks, kv_cols))
    )
    vmem = pl.BlockSpec(memory_space=pltpu.VMEM)
    return pl.pallas_call(
        partial(fused_kernel, ctx_size // 4, reach),
        out_shape=(
            jax.ShapeDtypeStruct((rows, q_cols), jnp.bfloat16),
            jax.ShapeDtypeStruct((rows, out_cols), jnp.bfloat16),
        ),
        in_specs=[vmem] * 4 + [pl.BlockSpec(memory_space=pl.ANY)],
        out_specs=(vmem, vmem),
        scratch_shapes=[
            pltpu.VMEM((ctx_size, 2 * rows + 16, kv_cols), jnp.bfloat16),
            pltpu.VMEM((kv_local, 2 * HDIM, group * rows), jnp.bfloat16),
            pltpu.VMEM((kv_local, HDIM, group * rows), jnp.float32),
            pltpu.VMEM((kv_local, 8, group * rows), jnp.float32),
            pltpu.VMEM((kv_local, 8, group * rows), jnp.float32),
            pltpu.VMEM(out_weight.shape, jnp.bfloat16),
            pltpu.VMEM((chunks, rows, width), jnp.bfloat16),
            pltpu.VMEM((chunks, rows, width), jnp.float32),
            pltpu.VMEM((chunks, rows, width), jnp.bfloat16),
            pltpu.SemaphoreType.DMA((3, ctx_size, 4)),
            pltpu.SemaphoreType.DMA((ctx_size, 4)),
            pltpu.SemaphoreType.DMA,
            pltpu.SemaphoreType.DMA((chunks,)),
            pltpu.SemaphoreType.DMA((chunks,)),
        ],
        compiler_params=pltpu.CompilerParams(
            collective_id=0, has_side_effects=True, vmem_limit_bytes=52 * 1024 * 1024
        ),
    )(query_rows, key_rows, value_rows, doc_tile, out_weight)


def solution(mesh):
    in_specs = (P("ctx", "hd"), P("ctx", "hd"), P("ctx", "hd"), P("ctx"), P("hd", None))
    out_specs = (P("ctx", "hd"), P("ctx", "hd"))
    body = per_device
    if mesh.shape["ctx"] == 16 and mesh.shape["hd"] == 2:
        body = partial(fused_device, mesh.shape["ctx"])
    return jax.shard_map(
        body, mesh=mesh, in_specs=in_specs, out_specs=out_specs, check_vma=False
    )
```

```python
from functools import partial
import math

import jax
import jax.numpy as jnp
from jax import lax
from jax.experimental import pallas as pl
from jax.experimental.pallas import tpu as pltpu
from jax.sharding import PartitionSpec as P

HDIM = 128
BLOCK = 64


NEG_BIG = -1e30


def attend_part(
    softmax_state, shard_part, leading_row, query_heads, query_pos, query_doc, score_scale
):
    key_part, value_part, doc_part = shard_part
    row_count = key_part.shape[0]
    block_len = 256
    kv_local = query_heads.shape[1]
    key_blocks = key_part.reshape(row_count // block_len, block_len, kv_local, HDIM)
    value_blocks = value_part.reshape(row_count // block_len, block_len, kv_local, HDIM)
    doc_blocks = doc_part.reshape(row_count // block_len, block_len)

    def one_block(block_index, running):
        block_keys = key_blocks[block_index]
        block_values = value_blocks[block_index]
        key_pos = block_index * block_len + jnp.arange(block_len, dtype=jnp.int32)
        visible = (key_pos[None, :] <= query_pos[:, None]) & (key_pos[None, :] >= 0)
        visible = visible & (doc_blocks[block_index][None, :] == query_doc[:, None])

        def compute(inner_state):
            old_max, old_sum, old_weighted = inner_state
            scores = (
                jnp.einsum(
                    "tkgd,skd->kgts", query_heads, block_keys, preferred_element_type=jnp.float32
                )
                * score_scale
            )
            scores = jnp.where(visible[None, None], scores, NEG_BIG)
            new_max = jnp.maximum(old_max, jnp.max(scores, axis=-1))
            factor = jnp.exp(old_max - new_max)
            weights = jnp.where(visible[None, None], jnp.exp(scores - new_max[..., None]), 0.0)
            new_sum = old_sum * factor + jnp.sum(weights, axis=-1)
            update = jnp.einsum(
                "kgts,skd->kgtd",
                weights.astype(jnp.bfloat16),
                block_values,
                preferred_element_type=jnp.float32,
            )
            return (new_max, new_sum, old_weighted * factor[..., None] + update)

        return lax.cond(jnp.any(visible), compute, lambda inner_state: inner_state, running)

    return lax.fori_loop(0, row_count // block_len, one_block, softmax_state)


def attention_part(query_rows, key_rows, value_rows, doc_ids):
    tokens_here = query_rows.shape[0]
    kv_local = key_rows.shape[1] // HDIM
    group_size = query_rows.shape[1] // key_rows.shape[1]
    position = lax.axis_index("ctx")
    query_heads = query_rows.reshape(tokens_here, kv_local, group_size, HDIM)
    query_pos = position * tokens_here + jnp.arange(tokens_here, dtype=jnp.int32)
    token_docs = jnp.repeat(doc_ids, BLOCK)
    fold_part = partial(
        attend_part,
        query_heads=query_heads,
        query_pos=query_pos,
        query_doc=token_docs,
        score_scale=1.0 / math.sqrt(HDIM),
    )
    start_state = (
        jnp.full((kv_local, group_size, tokens_here), NEG_BIG, jnp.float32),
        jnp.zeros((kv_local, group_size, tokens_here), jnp.float32),
        jnp.zeros((kv_local, group_size, tokens_here, HDIM), jnp.float32),
    )
    softmax_state = fold_part(
        start_state,
        (
            lax.all_gather(key_rows, "ctx", axis=0, tiled=True),
            lax.all_gather(value_rows, "ctx", axis=0, tiled=True),
            lax.all_gather(token_docs, "ctx", axis=0, tiled=True),
        ),
        jnp.int32(0),
    )
    final_max, final_sum, final_weighted = softmax_state
    attended = final_weighted / final_sum[..., None]
    return (
        attended.transpose(2, 0, 1, 3)
        .reshape(tokens_here, kv_local * group_size * HDIM)
        .astype(jnp.bfloat16)
    )


def per_device(query_rows, key_rows, value_rows, doc_ids, out_weight):
    attended = attention_part(query_rows, key_rows, value_rows, doc_ids)
    partial_proj = jnp.dot(attended, out_weight, preferred_element_type=jnp.float32)
    projected = lax.psum_scatter(
        partial_proj.astype(jnp.bfloat16), "hd", scatter_dimension=1, tiled=True
    )
    return (attended, projected)

NEG_MASK = -1e30
LOG2E = 1.4426950408889634
MESH = pl.DeviceIdType.MESH


def fused_kernel(
    levels, reach, q_hbm, k_ref, v_ref, doc_ref, w_ref, att_ref, proj_ref,
    q_ref, buf, qa, acc, mrow, lrow, wbuf, psend, pown, precv,
    send_sem, recv_sem, w_sem, in_sem, ysend_sem, yrecv_sem,
):
    rows = q_ref.shape[0]
    kv_local = k_ref.shape[1] // HDIM
    group = q_ref.shape[1] // k_ref.shape[1]
    scale = LOG2E / math.sqrt(HDIM)
    v_at = rows + 16
    me = lax.axis_index("ctx")
    half = lax.axis_index("hd")
    z, x, c = lax.div(me, 4), lax.rem(lax.div(me, 2), 2), lax.rem(me, 2)
    up, across, sibling = me + 4, 4 * z + 2 * (1 - x) + c, 4 * z + 2 * x + (1 - c)
    across_chip = 4 * z + 2 * (1 - x)

    k_copy = pltpu.make_async_copy(k_ref, buf.at[me, pl.ds(0, rows)], in_sem.at[0])
    v_copy = pltpu.make_async_copy(v_ref, buf.at[me, pl.ds(v_at, rows)], in_sem.at[1])
    q_copy = pltpu.make_async_copy(q_hbm, q_ref, in_sem.at[2])
    k_copy.start()
    v_copy.start()
    q_copy.start()
    w_copy = pltpu.make_async_copy(w_ref, wbuf, w_sem)
    w_copy.start()

    barrier = pltpu.get_barrier_semaphore()
    pl.semaphore_signal(barrier, inc=1, device_id={"ctx": across}, device_id_type=MESH)
    pl.semaphore_signal(barrier, inc=1, device_id={"ctx": sibling}, device_id_type=MESH)
    pl.semaphore_signal(barrier, inc=1, device_id={"hd": 1 - half}, device_id_type=MESH)

    @pl.when(z + 1 < levels)
    def _():
        pl.semaphore_signal(barrier, inc=1, device_id={"ctx": up}, device_id_type=MESH)

    @pl.when(z > 0)
    def _():
        pl.semaphore_signal(barrier, inc=1, device_id={"ctx": me - 4}, device_id_type=MESH)

    buf[me, rows:v_at, :] = doc_ref[...]
    k_copy.wait()
    v_copy.wait()

    pl.semaphore_wait(
        barrier, 3 + jnp.where(z + 1 < levels, 1, 0) + jnp.where(z > 0, 1, 0)
    )

    middle = rows // 2
    parts = (
        (0, middle), (middle, v_at - middle), (v_at, middle), (v_at + middle, rows - middle)
    )

    def copy(src, part, direction, target):
        ref = buf.at[src, pl.ds(parts[part][0], parts[part][1])]
        return pltpu.make_async_remote_copy(
            src_ref=ref, dst_ref=ref,
            send_sem=send_sem.at[direction, src, part],
            recv_sem=recv_sem.at[src, part],
            device_id={"ctx": target}, device_id_type=MESH,
        )

    def sends(src, column):
        return (
            (0, up, column & (z + 1 < levels) & (4 * (z + 1) - src <= reach)),
            (1, across, column & (src < across_chip) & (across_chip - src <= reach)),
            (2, sibling, (sibling > src) & (sibling - src <= reach)),
        )

    def forward(src, column, part):
        for direction, target, needed in sends(src, column):
            @pl.when(needed)
            def _():
                copy(src, part, direction, target).start()

    def drain(src, column):
        for direction, target, needed in sends(src, column):
            @pl.when(needed)
            def _():
                for part in range(len(parts)):
                    copy(src, part, direction, target).wait_send()

    always = me >= 0
    for part in range(len(parts)):
        forward(me, always, part)

    lane = lax.broadcasted_iota(jnp.int32, (1, rows), 1)
    docs = doc_ref[...].astype(jnp.float32)
    query_doc = jnp.zeros((1, rows), jnp.float32)
    for b in range(rows // BLOCK):
        inside = (lane >= b * BLOCK) & (lane < (b + 1) * BLOCK)
        query_doc = jnp.where(inside, docs[b : b + 1, 0:rows], query_doc)
    ids = lax.broadcasted_iota(jnp.int32, (HDIM, rows), 0).astype(jnp.float32)
    onehot = jnp.where(ids == query_doc, 1.0, 0.0).astype(jnp.bfloat16)
    q_copy.wait()
    for kv in range(kv_local):
        for g in range(group):
            head = (kv * group + g) * HDIM
            cols = slice(g * rows, (g + 1) * rows)
            qa[kv, 0:HDIM, cols] = q_ref[:, head : head + HDIM].T
            qa[kv, HDIM:, cols] = onehot

    def attend(src, diagonal):
        shard_docs = buf[src, rows:v_at, 0:HDIM].astype(jnp.float32)
        doc_lane = lax.broadcasted_iota(jnp.int32, (BLOCK, HDIM), 1).astype(jnp.float32)
        key_mask = jnp.concatenate(
            [
                jnp.where(doc_lane == shard_docs[b : b + 1, :], 0.0, NEG_MASK)
                for b in range(rows // BLOCK)
            ],
            axis=0,
        ).astype(jnp.bfloat16)

        heads = [(kv, g) for kv in range(kv_local) for g in range(group)]
        keys_of, values_of = {}, {}

        def scores_of(kv, g):
            if kv not in keys_of:
                at = slice(kv * HDIM, (kv + 1) * HDIM)
                keys_of[kv] = jnp.concatenate([buf[src, 0:rows, at], key_mask], axis=1)
                values_of[kv] = buf[src, v_at:, at].T
            scores = jnp.dot(
                keys_of[kv],
                qa[kv, :, g * rows : (g + 1) * rows],
                preferred_element_type=jnp.float32,
            )
            if diagonal:
                key_pos = lax.broadcasted_iota(jnp.int32, scores.shape, 0)
                query_pos = lax.broadcasted_iota(jnp.int32, scores.shape, 1)
                scores = jnp.where(key_pos <= query_pos, scores, NEG_MASK)
            return scores

        ahead = 2
        ready = [scores_of(*head) for head in heads[:ahead]]
        for index, (kv, g) in enumerate(heads):
            cols = slice(g * rows, (g + 1) * rows)
            scores = ready.pop(0)
            if index + ahead < len(heads):
                ready.append(scores_of(*heads[index + ahead]))
            top = jnp.max(scores, axis=0, keepdims=True)
            if not diagonal:
                old = mrow[kv, 0:1, cols]
                top = jnp.maximum(top, old)
                factor = jnp.exp2((old - top) * scale)
            weights = jnp.exp2((scores - top) * scale)
            total = jnp.sum(weights, axis=0, keepdims=True)
            update = jnp.dot(
                values_of[kv], weights.astype(jnp.bfloat16), preferred_element_type=jnp.float32
            )
            if not diagonal:
                total = total + lrow[kv, 0:1, cols] * factor
                update = update + acc[kv, :, cols] * factor
            mrow[kv, 0:1, cols] = top
            lrow[kv, 0:1, cols] = total
            acc[kv, :, cols] = update

    attend(me, True)

    def event(step):
        kind = lax.rem(step, 4)
        back = lax.div(step, 4) - jnp.where(kind >= 2, 1, 0)
        src_z = z - back
        src_x = jnp.where(kind >= 2, 1 - x, x)
        src_c = jnp.where(lax.rem(kind, 2) == 1, 1 - c, c)
        src = 4 * src_z + 2 * src_x + src_c
        near = (src < me) & (me - src <= reach)
        chip = 4 * z + 2 * x
        by_level = (kind == 0) & (back >= 1) & (4 * z - src <= reach)
        by_across = (kind == 2) & (src < chip) & (chip - src <= reach)
        by_sibling = (lax.rem(kind, 2) == 1) & near
        held = (back >= 0) & (src_z >= 0) & (by_level | by_across | by_sibling)
        return src, kind, held, held & near

    @pl.loop(0, 4 * (levels + 1))
    def _(step):
        src, kind, held, near = event(step)
        next_src, next_kind, next_held, _near = event(step + 1)
        odd = lax.rem(kind, 2) == 1

        @pl.when(odd & next_held)
        def _():
            for part in range(len(parts)):
                copy(next_src, part, 0, sibling).wait_recv()
                forward(next_src, next_kind == 0, part)

        @pl.when(odd & held)
        def _():
            for part in range(len(parts)):
                copy(src, part, 0, sibling).wait_recv()

        @pl.when(near)
        def _():
            attend(src, False)

    @pl.loop(0, kv_local)
    def _(kv):
        for g in range(group):
            cols = slice(g * rows, (g + 1) * rows)
            head = acc[kv, :, cols] / lrow[kv, 0:1, cols]
            at = pl.ds(pl.multiple_of((kv * group + g) * HDIM, HDIM), HDIM)
            att_ref[:, at] = head.T.astype(jnp.bfloat16)

    w_copy.wait()
    chunks, _, width = psend.shape

    def exchange(n):
        return pltpu.make_async_remote_copy(
            src_ref=psend.at[n], dst_ref=precv.at[n],
            send_sem=ysend_sem.at[n], recv_sem=yrecv_sem.at[n],
            device_id={"hd": 1 - half}, device_id_type=MESH,
        )

    def project(first, n):
        at = pl.ds(pl.multiple_of((first * chunks + n) * width, width), width)
        return jnp.dot(att_ref[...], wbuf[:, at], preferred_element_type=jnp.float32)

    @pl.loop(0, chunks)
    def _(n):
        psend[n] = project(1 - half, n).astype(jnp.bfloat16)
        exchange(n).start()

    @pl.loop(0, chunks)
    def _(n):
        pown[n] = project(half, n)

    for n in range(chunks):
        exchange(n).wait_recv()
        proj_ref[:, n * width : (n + 1) * width] = (
            pown[n] + precv[n].astype(jnp.float32)
        ).astype(jnp.bfloat16)

    for n in range(chunks):
        exchange(n).wait_send()
    drain(me, always)

    @pl.loop(0, 4 * (levels + 1))
    def _(step):
        src, kind, held, _near = event(step)

        @pl.when(held & (lax.rem(kind, 2) == 0))
        def _():
            drain(src, kind == 0)


def fused_device(ctx_size, query_rows, key_rows, value_rows, doc_ids, out_weight):
    rows, q_cols = query_rows.shape
    kv_cols = key_rows.shape[1]
    kv_local = kv_cols // HDIM
    group = q_cols // kv_cols
    shard_blocks = rows // BLOCK
    reach = -(-(ctx_size * shard_blocks * 5 // 8 - 1) // shard_blocks)
    width = 512
    out_cols = out_weight.shape[1] // 2
    chunks = out_cols // width
    doc_tile = jnp.zeros((16, kv_cols), jnp.bfloat16).at[0:shard_blocks].set(
        jnp.broadcast_to(doc_ids.astype(jnp.bfloat16)[:, None], (shard_blocks, kv_cols))
    )
    vmem = pl.BlockSpec(memory_space=pltpu.VMEM)
    hbm = pl.BlockSpec(memory_space=pltpu.HBM)
    return pl.pallas_call(
        partial(fused_kernel, ctx_size // 4, reach),
        out_shape=(
            jax.ShapeDtypeStruct((rows, q_cols), jnp.bfloat16),
            jax.ShapeDtypeStruct((rows, out_cols), jnp.bfloat16),
        ),
        in_specs=[hbm, hbm, hbm, vmem, hbm],
        out_specs=(vmem, vmem),
        scratch_shapes=[
            pltpu.VMEM((rows, q_cols), jnp.bfloat16),
            pltpu.VMEM((ctx_size, 2 * rows + 16, kv_cols), jnp.bfloat16),
            pltpu.VMEM((kv_local, 2 * HDIM, group * rows), jnp.bfloat16),
            pltpu.VMEM((kv_local, HDIM, group * rows), jnp.float32),
            pltpu.VMEM((kv_local, 8, group * rows), jnp.float32),
            pltpu.VMEM((kv_local, 8, group * rows), jnp.float32),
            pltpu.VMEM(out_weight.shape, jnp.bfloat16),
            pltpu.VMEM((chunks, rows, width), jnp.bfloat16),
            pltpu.VMEM((chunks, rows, width), jnp.float32),
            pltpu.VMEM((chunks, rows, width), jnp.bfloat16),
            pltpu.SemaphoreType.DMA((3, ctx_size, 4)),
            pltpu.SemaphoreType.DMA((ctx_size, 4)),
            pltpu.SemaphoreType.DMA,
            pltpu.SemaphoreType.DMA((3,)),
            pltpu.SemaphoreType.DMA((chunks,)),
            pltpu.SemaphoreType.DMA((chunks,)),
        ],
        compiler_params=pltpu.CompilerParams(
            collective_id=0, has_side_effects=True, vmem_limit_bytes=44 * 1024 * 1024
        ),
    )(query_rows, key_rows, value_rows, doc_tile, out_weight)


def solution(mesh):
    in_specs = (P("ctx", "hd"), P("ctx", "hd"), P("ctx", "hd"), P("ctx"), P("hd", None))
    out_specs = (P("ctx", "hd"), P("ctx", "hd"))
    body = per_device
    if mesh.shape["ctx"] == 16 and mesh.shape["hd"] == 2:
        body = partial(fused_device, mesh.shape["ctx"])
    return jax.shard_map(
        body, mesh=mesh, in_specs=in_specs, out_specs=out_specs, check_vma=False
    )
```

```python
from functools import partial
import math

import jax
import jax.numpy as jnp
from jax import lax
from jax.experimental import pallas as pl
from jax.experimental.pallas import tpu as pltpu
from jax.sharding import PartitionSpec as P

HDIM = 128
BLOCK = 64


NEG_BIG = -1e30


def attend_part(
    softmax_state, shard_part, leading_row, query_heads, query_pos, query_doc, score_scale
):
    key_part, value_part, doc_part = shard_part
    row_count = key_part.shape[0]
    block_len = 256
    kv_local = query_heads.shape[1]
    key_blocks = key_part.reshape(row_count // block_len, block_len, kv_local, HDIM)
    value_blocks = value_part.reshape(row_count // block_len, block_len, kv_local, HDIM)
    doc_blocks = doc_part.reshape(row_count // block_len, block_len)

    def one_block(block_index, running):
        block_keys = key_blocks[block_index]
        block_values = value_blocks[block_index]
        key_pos = block_index * block_len + jnp.arange(block_len, dtype=jnp.int32)
        visible = (key_pos[None, :] <= query_pos[:, None]) & (key_pos[None, :] >= 0)
        visible = visible & (doc_blocks[block_index][None, :] == query_doc[:, None])

        def compute(inner_state):
            old_max, old_sum, old_weighted = inner_state
            scores = (
                jnp.einsum(
                    "tkgd,skd->kgts", query_heads, block_keys, preferred_element_type=jnp.float32
                )
                * score_scale
            )
            scores = jnp.where(visible[None, None], scores, NEG_BIG)
            new_max = jnp.maximum(old_max, jnp.max(scores, axis=-1))
            factor = jnp.exp(old_max - new_max)
            weights = jnp.where(visible[None, None], jnp.exp(scores - new_max[..., None]), 0.0)
            new_sum = old_sum * factor + jnp.sum(weights, axis=-1)
            update = jnp.einsum(
                "kgts,skd->kgtd",
                weights.astype(jnp.bfloat16),
                block_values,
                preferred_element_type=jnp.float32,
            )
            return (new_max, new_sum, old_weighted * factor[..., None] + update)

        return lax.cond(jnp.any(visible), compute, lambda inner_state: inner_state, running)

    return lax.fori_loop(0, row_count // block_len, one_block, softmax_state)


def attention_part(query_rows, key_rows, value_rows, doc_ids):
    tokens_here = query_rows.shape[0]
    kv_local = key_rows.shape[1] // HDIM
    group_size = query_rows.shape[1] // key_rows.shape[1]
    position = lax.axis_index("ctx")
    query_heads = query_rows.reshape(tokens_here, kv_local, group_size, HDIM)
    query_pos = position * tokens_here + jnp.arange(tokens_here, dtype=jnp.int32)
    token_docs = jnp.repeat(doc_ids, BLOCK)
    fold_part = partial(
        attend_part,
        query_heads=query_heads,
        query_pos=query_pos,
        query_doc=token_docs,
        score_scale=1.0 / math.sqrt(HDIM),
    )
    start_state = (
        jnp.full((kv_local, group_size, tokens_here), NEG_BIG, jnp.float32),
        jnp.zeros((kv_local, group_size, tokens_here), jnp.float32),
        jnp.zeros((kv_local, group_size, tokens_here, HDIM), jnp.float32),
    )
    softmax_state = fold_part(
        start_state,
        (
            lax.all_gather(key_rows, "ctx", axis=0, tiled=True),
            lax.all_gather(value_rows, "ctx", axis=0, tiled=True),
            lax.all_gather(token_docs, "ctx", axis=0, tiled=True),
        ),
        jnp.int32(0),
    )
    final_max, final_sum, final_weighted = softmax_state
    attended = final_weighted / final_sum[..., None]
    return (
        attended.transpose(2, 0, 1, 3)
        .reshape(tokens_here, kv_local * group_size * HDIM)
        .astype(jnp.bfloat16)
    )


def per_device(query_rows, key_rows, value_rows, doc_ids, out_weight):
    attended = attention_part(query_rows, key_rows, value_rows, doc_ids)
    partial_proj = jnp.dot(attended, out_weight, preferred_element_type=jnp.float32)
    projected = lax.psum_scatter(
        partial_proj.astype(jnp.bfloat16), "hd", scatter_dimension=1, tiled=True
    )
    return (attended, projected)

NEG_MASK = -1e30
LOG2E = 1.4426950408889634
MESH = pl.DeviceIdType.MESH


def fused_kernel(
    levels, reach, q_hbm, k_ref, v_ref, doc_ref, w_ref, att_ref, proj_ref,
    q_ref, buf, qa, acc, mrow, lrow, wbuf, psend, pown, precv,
    send_sem, recv_sem, w_sem, in_sem, ysend_sem, yrecv_sem,
):
    rows = q_ref.shape[0]
    kv_local = k_ref.shape[1] // HDIM
    group = q_ref.shape[1] // k_ref.shape[1]
    scale = LOG2E / math.sqrt(HDIM)
    v_at = rows + 16
    me = lax.axis_index("ctx")
    half = lax.axis_index("hd")
    z, x, c = lax.div(me, 4), lax.rem(lax.div(me, 2), 2), lax.rem(me, 2)
    up, across, sibling = me + 4, 4 * z + 2 * (1 - x) + c, 4 * z + 2 * x + (1 - c)
    across_chip = 4 * z + 2 * (1 - x)

    k_copy = pltpu.make_async_copy(k_ref, buf.at[me, pl.ds(0, rows)], in_sem.at[0])
    v_copy = pltpu.make_async_copy(v_ref, buf.at[me, pl.ds(v_at, rows)], in_sem.at[1])
    q_copy = pltpu.make_async_copy(q_hbm, q_ref, in_sem.at[2])
    k_copy.start()
    v_copy.start()
    q_copy.start()
    w_copy = pltpu.make_async_copy(w_ref, wbuf, w_sem)
    w_copy.start()

    barrier = pltpu.get_barrier_semaphore()
    pl.semaphore_signal(barrier, inc=1, device_id={"ctx": across}, device_id_type=MESH)
    pl.semaphore_signal(barrier, inc=1, device_id={"ctx": sibling}, device_id_type=MESH)
    pl.semaphore_signal(barrier, inc=1, device_id={"hd": 1 - half}, device_id_type=MESH)

    @pl.when(z + 1 < levels)
    def _():
        pl.semaphore_signal(barrier, inc=1, device_id={"ctx": up}, device_id_type=MESH)

    @pl.when(z > 0)
    def _():
        pl.semaphore_signal(barrier, inc=1, device_id={"ctx": me - 4}, device_id_type=MESH)

    buf[me, rows:v_at, :] = doc_ref[...]
    k_copy.wait()
    v_copy.wait()

    pl.semaphore_wait(
        barrier, 3 + jnp.where(z + 1 < levels, 1, 0) + jnp.where(z > 0, 1, 0)
    )

    middle = rows // 2
    parts = (
        (0, middle), (middle, v_at - middle), (v_at, middle), (v_at + middle, rows - middle)
    )

    def copy(src, part, direction, target):
        ref = buf.at[src, pl.ds(parts[part][0], parts[part][1])]
        return pltpu.make_async_remote_copy(
            src_ref=ref, dst_ref=ref,
            send_sem=send_sem.at[direction, src, part],
            recv_sem=recv_sem.at[src, part],
            device_id={"ctx": target}, device_id_type=MESH,
        )

    def sends(src, column, part):
        levels_down = z - lax.div(src, 4)
        by_column = column & (4 * (z + 1) - src <= reach)
        crossing = column & (src < across_chip) & (across_chip - src <= reach)
        if part >= 2:
            by_other = jnp.logical_not(column) & (levels_down == 2)
            by_column = (by_column | by_other) & (up - src <= reach)
            crossing = crossing & (levels_down < 3)
        return (
            (0, up, by_column & (z + 1 < levels)),
            (1, across, crossing),
            (2, sibling, (sibling > src) & (sibling - src <= reach)),
        )

    def forward(src, column, part):
        for direction, target, needed in sends(src, column, part):
            @pl.when(needed)
            def _():
                copy(src, part, direction, target).start()

    def drain(src, column):
        for part in range(len(parts)):
            for direction, target, needed in sends(src, column, part):
                @pl.when(needed)
                def _():
                    copy(src, part, direction, target).wait_send()

    always = me >= 0
    for part in range(len(parts)):
        forward(me, always, part)

    lane = lax.broadcasted_iota(jnp.int32, (1, rows), 1)
    docs = doc_ref[...].astype(jnp.float32)
    query_doc = jnp.zeros((1, rows), jnp.float32)
    for b in range(rows // BLOCK):
        inside = (lane >= b * BLOCK) & (lane < (b + 1) * BLOCK)
        query_doc = jnp.where(inside, docs[b : b + 1, 0:rows], query_doc)
    ids = lax.broadcasted_iota(jnp.int32, (HDIM, rows), 0).astype(jnp.float32)
    onehot = jnp.where(ids == query_doc, 1.0, 0.0).astype(jnp.bfloat16)
    q_copy.wait()
    for kv in range(kv_local):
        for g in range(group):
            head = (kv * group + g) * HDIM
            cols = slice(g * rows, (g + 1) * rows)
            qa[kv, 0:HDIM, cols] = q_ref[:, head : head + HDIM].T
            qa[kv, HDIM:, cols] = onehot

    def attend(src, diagonal):
        shard_docs = buf[src, rows:v_at, 0:HDIM].astype(jnp.float32)
        doc_lane = lax.broadcasted_iota(jnp.int32, (BLOCK, HDIM), 1).astype(jnp.float32)
        key_mask = jnp.concatenate(
            [
                jnp.where(doc_lane == shard_docs[b : b + 1, :], 0.0, NEG_MASK)
                for b in range(rows // BLOCK)
            ],
            axis=0,
        ).astype(jnp.bfloat16)

        heads = [(kv, g) for kv in range(kv_local) for g in range(group)]
        keys_of, values_of = {}, {}

        def scores_of(kv, g):
            if kv not in keys_of:
                at = slice(kv * HDIM, (kv + 1) * HDIM)
                keys_of[kv] = jnp.concatenate([buf[src, 0:rows, at], key_mask], axis=1)
                values_of[kv] = buf[src, v_at:, at].T
            scores = jnp.dot(
                keys_of[kv],
                qa[kv, :, g * rows : (g + 1) * rows],
                preferred_element_type=jnp.float32,
            )
            if diagonal:
                key_pos = lax.broadcasted_iota(jnp.int32, scores.shape, 0)
                query_pos = lax.broadcasted_iota(jnp.int32, scores.shape, 1)
                scores = jnp.where(key_pos <= query_pos, scores, NEG_MASK)
            return scores

        ahead = 2
        ready = [scores_of(*head) for head in heads[:ahead]]
        for index, (kv, g) in enumerate(heads):
            cols = slice(g * rows, (g + 1) * rows)
            scores = ready.pop(0)
            if index + ahead < len(heads):
                ready.append(scores_of(*heads[index + ahead]))
            top = jnp.max(scores, axis=0, keepdims=True)
            if not diagonal:
                old = mrow[kv, 0:1, cols]
                top = jnp.maximum(top, old)
                factor = jnp.exp2((old - top) * scale)
            weights = jnp.exp2((scores - top) * scale)
            total = jnp.sum(weights, axis=0, keepdims=True)
            update = jnp.dot(
                values_of[kv], weights.astype(jnp.bfloat16), preferred_element_type=jnp.float32
            )
            if not diagonal:
                total = total + lrow[kv, 0:1, cols] * factor
                update = update + acc[kv, :, cols] * factor
            mrow[kv, 0:1, cols] = top
            lrow[kv, 0:1, cols] = total
            acc[kv, :, cols] = update

    attend(me, True)

    def event(step):
        kind = lax.rem(step, 4)
        back = lax.div(step, 4) - jnp.where(kind >= 2, 1, 0)
        src_z = z - back
        src_x = jnp.where(kind >= 2, 1 - x, x)
        src_c = jnp.where(lax.rem(kind, 2) == 1, 1 - c, c)
        src = 4 * src_z + 2 * src_x + src_c
        near = (src < me) & (me - src <= reach)
        chip = 4 * z + 2 * x
        by_level = (kind == 0) & (back >= 1) & (4 * z - src <= reach)
        by_across = (kind == 2) & (src < chip) & (chip - src <= reach)
        by_sibling = (lax.rem(kind, 2) == 1) & near
        held = (back >= 0) & (src_z >= 0) & (by_level | by_across | by_sibling)
        return src, kind, held, held & near

    @pl.loop(0, 4 * (levels + 1))
    def _(step):
        src, kind, held, near = event(step)
        next_src, next_kind, next_held, next_near = event(step + 1)
        odd = lax.rem(kind, 2) == 1

        @pl.when(odd & next_held)
        def _():
            for part in range(len(parts)):
                @pl.when(next_near | (part < 2))
                def _():
                    copy(next_src, part, 0, sibling).wait_recv()
                    forward(next_src, next_kind == 0, part)

        @pl.when(odd & held)
        def _():
            for part in range(len(parts)):
                copy(src, part, 0, sibling).wait_recv()

        @pl.when(near)
        def _():
            attend(src, False)

    @pl.loop(0, kv_local)
    def _(kv):
        for g in range(group):
            cols = slice(g * rows, (g + 1) * rows)
            head = acc[kv, :, cols] / lrow[kv, 0:1, cols]
            at = pl.ds(pl.multiple_of((kv * group + g) * HDIM, HDIM), HDIM)
            att_ref[:, at] = head.T.astype(jnp.bfloat16)

    w_copy.wait()
    chunks, _, width = psend.shape

    def exchange(n):
        return pltpu.make_async_remote_copy(
            src_ref=psend.at[n], dst_ref=precv.at[n],
            send_sem=ysend_sem.at[n], recv_sem=yrecv_sem.at[n],
            device_id={"hd": 1 - half}, device_id_type=MESH,
        )

    def project(first, n):
        at = pl.ds(pl.multiple_of((first * chunks + n) * width, width), width)
        return jnp.dot(att_ref[...], wbuf[:, at], preferred_element_type=jnp.float32)

    @pl.loop(0, chunks)
    def _(n):
        psend[n] = project(1 - half, n).astype(jnp.bfloat16)
        exchange(n).start()

    @pl.loop(0, chunks)
    def _(n):
        pown[n] = project(half, n)

    for n in range(chunks):
        exchange(n).wait_recv()
        proj_ref[:, n * width : (n + 1) * width] = (
            pown[n] + precv[n].astype(jnp.float32)
        ).astype(jnp.bfloat16)

    for n in range(chunks):
        exchange(n).wait_send()
    drain(me, always)

    @pl.loop(0, 4 * (levels + 1))
    def _(step):
        src, kind, held, _near = event(step)

        @pl.when(held & (lax.rem(kind, 2) == 0))
        def _():
            drain(src, kind == 0)


def fused_device(ctx_size, query_rows, key_rows, value_rows, doc_ids, out_weight):
    rows, q_cols = query_rows.shape
    kv_cols = key_rows.shape[1]
    kv_local = kv_cols // HDIM
    group = q_cols // kv_cols
    shard_blocks = rows // BLOCK
    reach = -(-(ctx_size * shard_blocks * 5 // 8 - 1) // shard_blocks)
    width = 512
    out_cols = out_weight.shape[1] // 2
    chunks = out_cols // width
    doc_tile = jnp.zeros((16, kv_cols), jnp.bfloat16).at[0:shard_blocks].set(
        jnp.broadcast_to(doc_ids.astype(jnp.bfloat16)[:, None], (shard_blocks, kv_cols))
    )
    vmem = pl.BlockSpec(memory_space=pltpu.VMEM)
    hbm = pl.BlockSpec(memory_space=pltpu.HBM)
    return pl.pallas_call(
        partial(fused_kernel, ctx_size // 4, reach),
        out_shape=(
            jax.ShapeDtypeStruct((rows, q_cols), jnp.bfloat16),
            jax.ShapeDtypeStruct((rows, out_cols), jnp.bfloat16),
        ),
        in_specs=[hbm, hbm, hbm, vmem, hbm],
        out_specs=(vmem, vmem),
        scratch_shapes=[
            pltpu.VMEM((rows, q_cols), jnp.bfloat16),
            pltpu.VMEM((ctx_size, 2 * rows + 16, kv_cols), jnp.bfloat16),
            pltpu.VMEM((kv_local, 2 * HDIM, group * rows), jnp.bfloat16),
            pltpu.VMEM((kv_local, HDIM, group * rows), jnp.float32),
            pltpu.VMEM((kv_local, 8, group * rows), jnp.float32),
            pltpu.VMEM((kv_local, 8, group * rows), jnp.float32),
            pltpu.VMEM(out_weight.shape, jnp.bfloat16),
            pltpu.VMEM((chunks, rows, width), jnp.bfloat16),
            pltpu.VMEM((chunks, rows, width), jnp.float32),
            pltpu.VMEM((chunks, rows, width), jnp.bfloat16),
            pltpu.SemaphoreType.DMA((3, ctx_size, 4)),
            pltpu.SemaphoreType.DMA((ctx_size, 4)),
            pltpu.SemaphoreType.DMA,
            pltpu.SemaphoreType.DMA((3,)),
            pltpu.SemaphoreType.DMA((chunks,)),
            pltpu.SemaphoreType.DMA((chunks,)),
        ],
        compiler_params=pltpu.CompilerParams(
            collective_id=0, has_side_effects=True, vmem_limit_bytes=44 * 1024 * 1024
        ),
    )(query_rows, key_rows, value_rows, doc_tile, out_weight)


def solution(mesh):
    in_specs = (P("ctx", "hd"), P("ctx", "hd"), P("ctx", "hd"), P("ctx"), P("hd", None))
    out_specs = (P("ctx", "hd"), P("ctx", "hd"))
    body = per_device
    if mesh.shape["ctx"] == 16 and mesh.shape["hd"] == 2:
        body = partial(fused_device, mesh.shape["ctx"])
    return jax.shard_map(
        body, mesh=mesh, in_specs=in_specs, out_specs=out_specs, check_vma=False
    )
```

```python
from functools import partial
import math

import jax
import jax.numpy as jnp
from jax import lax
from jax.experimental import pallas as pl
from jax.experimental.pallas import tpu as pltpu
from jax.sharding import PartitionSpec as P

HDIM = 128
BLOCK = 64


NEG_BIG = -1e30


def attend_part(
    softmax_state, shard_part, leading_row, query_heads, query_pos, query_doc, score_scale
):
    key_part, value_part, doc_part = shard_part
    row_count = key_part.shape[0]
    block_len = 256
    kv_local = query_heads.shape[1]
    key_blocks = key_part.reshape(row_count // block_len, block_len, kv_local, HDIM)
    value_blocks = value_part.reshape(row_count // block_len, block_len, kv_local, HDIM)
    doc_blocks = doc_part.reshape(row_count // block_len, block_len)

    def one_block(block_index, running):
        block_keys = key_blocks[block_index]
        block_values = value_blocks[block_index]
        key_pos = block_index * block_len + jnp.arange(block_len, dtype=jnp.int32)
        visible = (key_pos[None, :] <= query_pos[:, None]) & (key_pos[None, :] >= 0)
        visible = visible & (doc_blocks[block_index][None, :] == query_doc[:, None])

        def compute(inner_state):
            old_max, old_sum, old_weighted = inner_state
            scores = (
                jnp.einsum(
                    "tkgd,skd->kgts", query_heads, block_keys, preferred_element_type=jnp.float32
                )
                * score_scale
            )
            scores = jnp.where(visible[None, None], scores, NEG_BIG)
            new_max = jnp.maximum(old_max, jnp.max(scores, axis=-1))
            factor = jnp.exp(old_max - new_max)
            weights = jnp.where(visible[None, None], jnp.exp(scores - new_max[..., None]), 0.0)
            new_sum = old_sum * factor + jnp.sum(weights, axis=-1)
            update = jnp.einsum(
                "kgts,skd->kgtd",
                weights.astype(jnp.bfloat16),
                block_values,
                preferred_element_type=jnp.float32,
            )
            return (new_max, new_sum, old_weighted * factor[..., None] + update)

        return lax.cond(jnp.any(visible), compute, lambda inner_state: inner_state, running)

    return lax.fori_loop(0, row_count // block_len, one_block, softmax_state)


def attention_part(query_rows, key_rows, value_rows, doc_ids):
    tokens_here = query_rows.shape[0]
    kv_local = key_rows.shape[1] // HDIM
    group_size = query_rows.shape[1] // key_rows.shape[1]
    position = lax.axis_index("ctx")
    query_heads = query_rows.reshape(tokens_here, kv_local, group_size, HDIM)
    query_pos = position * tokens_here + jnp.arange(tokens_here, dtype=jnp.int32)
    token_docs = jnp.repeat(doc_ids, BLOCK)
    fold_part = partial(
        attend_part,
        query_heads=query_heads,
        query_pos=query_pos,
        query_doc=token_docs,
        score_scale=1.0 / math.sqrt(HDIM),
    )
    start_state = (
        jnp.full((kv_local, group_size, tokens_here), NEG_BIG, jnp.float32),
        jnp.zeros((kv_local, group_size, tokens_here), jnp.float32),
        jnp.zeros((kv_local, group_size, tokens_here, HDIM), jnp.float32),
    )
    softmax_state = fold_part(
        start_state,
        (
            lax.all_gather(key_rows, "ctx", axis=0, tiled=True),
            lax.all_gather(value_rows, "ctx", axis=0, tiled=True),
            lax.all_gather(token_docs, "ctx", axis=0, tiled=True),
        ),
        jnp.int32(0),
    )
    final_max, final_sum, final_weighted = softmax_state
    attended = final_weighted / final_sum[..., None]
    return (
        attended.transpose(2, 0, 1, 3)
        .reshape(tokens_here, kv_local * group_size * HDIM)
        .astype(jnp.bfloat16)
    )


def per_device(query_rows, key_rows, value_rows, doc_ids, out_weight):
    attended = attention_part(query_rows, key_rows, value_rows, doc_ids)
    partial_proj = jnp.dot(attended, out_weight, preferred_element_type=jnp.float32)
    projected = lax.psum_scatter(
        partial_proj.astype(jnp.bfloat16), "hd", scatter_dimension=1, tiled=True
    )
    return (attended, projected)

NEG_MASK = -1e30
LOG2E = 1.4426950408889634
MESH = pl.DeviceIdType.MESH


def fused_kernel(
    levels, reach, q_hbm, k_ref, v_ref, doc_ref, w_ref, att_ref, proj_ref,
    q_ref, buf, qa, acc, mrow, lrow, wbuf, psend, pown, precv,
    send_sem, recv_sem, w_sem, in_sem, ysend_sem, yrecv_sem,
):
    rows = q_ref.shape[0]
    kv_local = k_ref.shape[1] // HDIM
    group = q_ref.shape[1] // k_ref.shape[1]
    scale = LOG2E / math.sqrt(HDIM)
    v_at = rows + 16
    me = lax.axis_index("ctx")
    half = lax.axis_index("hd")
    z, x, c = lax.div(me, 4), lax.rem(lax.div(me, 2), 2), lax.rem(me, 2)
    up, across, sibling = me + 4, 4 * z + 2 * (1 - x) + c, 4 * z + 2 * x + (1 - c)
    across_chip = 4 * z + 2 * (1 - x)

    k_copy = pltpu.make_async_copy(k_ref, buf.at[me, pl.ds(0, rows)], in_sem.at[0])
    v_copy = pltpu.make_async_copy(v_ref, buf.at[me, pl.ds(v_at, rows)], in_sem.at[1])
    q_copy = pltpu.make_async_copy(q_hbm, q_ref, in_sem.at[2])
    k_copy.start()
    v_copy.start()
    q_copy.start()
    w_copy = pltpu.make_async_copy(w_ref, wbuf, w_sem)
    w_copy.start()

    barrier = pltpu.get_barrier_semaphore()
    pl.semaphore_signal(barrier, inc=1, device_id={"ctx": across}, device_id_type=MESH)
    pl.semaphore_signal(barrier, inc=1, device_id={"ctx": sibling}, device_id_type=MESH)
    pl.semaphore_signal(barrier, inc=1, device_id={"hd": 1 - half}, device_id_type=MESH)

    @pl.when(z + 1 < levels)
    def _():
        pl.semaphore_signal(barrier, inc=1, device_id={"ctx": up}, device_id_type=MESH)

    @pl.when(z > 0)
    def _():
        pl.semaphore_signal(barrier, inc=1, device_id={"ctx": me - 4}, device_id_type=MESH)

    buf[me, rows:v_at, :] = doc_ref[...]
    k_copy.wait()
    v_copy.wait()

    pl.semaphore_wait(
        barrier, 3 + jnp.where(z + 1 < levels, 1, 0) + jnp.where(z > 0, 1, 0)
    )

    middle = rows // 2
    parts = (
        (0, middle), (middle, v_at - middle), (v_at, middle), (v_at + middle, rows - middle)
    )

    def copy(src, part, direction, target):
        ref = buf.at[src, pl.ds(parts[part][0], parts[part][1])]
        return pltpu.make_async_remote_copy(
            src_ref=ref, dst_ref=ref,
            send_sem=send_sem.at[direction, src, part],
            recv_sem=recv_sem.at[src, part],
            device_id={"ctx": target}, device_id_type=MESH,
        )

    def sends(src, column, part):
        levels_down = z - lax.div(src, 4)
        by_column = column & (4 * (z + 1) - src <= reach)
        crossing = column & (src < across_chip) & (across_chip - src <= reach)
        if part >= 2:
            by_other = jnp.logical_not(column) & (levels_down == 2)
            by_column = (by_column | by_other) & (up - src <= reach)
            crossing = crossing & (levels_down < 3)
        return (
            (0, up, by_column & (z + 1 < levels)),
            (1, across, crossing),
            (2, sibling, (sibling > src) & (sibling - src <= reach)),
        )

    def forward(src, column, part):
        for direction, target, needed in sends(src, column, part):
            @pl.when(needed)
            def _():
                copy(src, part, direction, target).start()

    def drain(src, column):
        for part in range(len(parts)):
            for direction, target, needed in sends(src, column, part):
                @pl.when(needed)
                def _():
                    copy(src, part, direction, target).wait_send()

    always = me >= 0
    for part in range(len(parts)):
        forward(me, always, part)

    lane = lax.broadcasted_iota(jnp.int32, (1, rows), 1)
    docs = doc_ref[...].astype(jnp.float32)
    query_doc = jnp.zeros((1, rows), jnp.float32)
    for b in range(rows // BLOCK):
        inside = (lane >= b * BLOCK) & (lane < (b + 1) * BLOCK)
        query_doc = jnp.where(inside, docs[b : b + 1, 0:rows], query_doc)
    ids = lax.broadcasted_iota(jnp.int32, (HDIM, rows), 0).astype(jnp.float32)
    onehot = jnp.where(ids == query_doc, 1.0, 0.0).astype(jnp.bfloat16)
    q_copy.wait()
    for kv in range(kv_local):
        for g in range(group):
            head = (kv * group + g) * HDIM
            cols = slice(g * rows, (g + 1) * rows)
            qa[kv, 0:HDIM, cols] = q_ref[:, head : head + HDIM].T
            qa[kv, HDIM:, cols] = onehot

    def attend(src, diagonal):
        shard_docs = buf[src, rows:v_at, 0:HDIM].astype(jnp.float32)
        doc_lane = lax.broadcasted_iota(jnp.int32, (BLOCK, HDIM), 1).astype(jnp.float32)
        key_mask = jnp.concatenate(
            [
                jnp.where(doc_lane == shard_docs[b : b + 1, :], 0.0, NEG_MASK)
                for b in range(rows // BLOCK)
            ],
            axis=0,
        ).astype(jnp.bfloat16)

        heads = [(kv, g) for kv in range(kv_local) for g in range(group)]
        keys_of, values_of = {}, {}
        ones = jnp.ones((16, rows), jnp.bfloat16)

        def scores_of(kv, g):
            if kv not in keys_of:
                at = slice(kv * HDIM, (kv + 1) * HDIM)
                keys_of[kv] = jnp.concatenate([buf[src, 0:rows, at], key_mask], axis=1)
                values_of[kv] = jnp.concatenate([buf[src, v_at:, at].T, ones], axis=0)
            scores = jnp.dot(
                keys_of[kv],
                qa[kv, :, g * rows : (g + 1) * rows],
                preferred_element_type=jnp.float32,
            )
            if diagonal:
                key_pos = lax.broadcasted_iota(jnp.int32, scores.shape, 0)
                query_pos = lax.broadcasted_iota(jnp.int32, scores.shape, 1)
                scores = jnp.where(key_pos <= query_pos, scores, NEG_MASK)
            return scores

        ahead = 2
        ready = [scores_of(*head) for head in heads[:ahead]]
        for index, (kv, g) in enumerate(heads):
            cols = slice(g * rows, (g + 1) * rows)
            scores = ready.pop(0)
            if index + ahead < len(heads):
                ready.append(scores_of(*heads[index + ahead]))
            top = jnp.max(scores, axis=0, keepdims=True)
            if not diagonal:
                old = mrow[kv, 0:1, cols]
                top = jnp.maximum(top, old)
                factor = jnp.exp2((old - top) * scale)
            weights = jnp.exp2((scores - top) * scale)
            summed = jnp.dot(
                values_of[kv], weights.astype(jnp.bfloat16), preferred_element_type=jnp.float32
            )
            update, total = summed[0:HDIM], summed[HDIM : HDIM + 1]
            if not diagonal:
                total = total + lrow[kv, 0:1, cols] * factor
                update = update + acc[kv, :, cols] * factor
            mrow[kv, 0:1, cols] = top
            lrow[kv, 0:1, cols] = total
            acc[kv, :, cols] = update

    attend(me, True)

    def event(step):
        kind = lax.rem(step, 4)
        back = lax.div(step, 4) - jnp.where(kind >= 2, 1, 0)
        src_z = z - back
        src_x = jnp.where(kind >= 2, 1 - x, x)
        src_c = jnp.where(lax.rem(kind, 2) == 1, 1 - c, c)
        src = 4 * src_z + 2 * src_x + src_c
        near = (src < me) & (me - src <= reach)
        chip = 4 * z + 2 * x
        by_level = (kind == 0) & (back >= 1) & (4 * z - src <= reach)
        by_across = (kind == 2) & (src < chip) & (chip - src <= reach)
        by_sibling = (lax.rem(kind, 2) == 1) & near
        held = (back >= 0) & (src_z >= 0) & (by_level | by_across | by_sibling)
        return src, kind, held, held & near

    @pl.loop(0, 4 * (levels + 1))
    def _(step):
        src, kind, held, near = event(step)
        next_src, next_kind, next_held, next_near = event(step + 1)
        odd = lax.rem(kind, 2) == 1

        @pl.when(odd & next_held)
        def _():
            for part in range(len(parts)):
                @pl.when(next_near | (part < 2))
                def _():
                    copy(next_src, part, 0, sibling).wait_recv()
                    forward(next_src, next_kind == 0, part)

        @pl.when(odd & held)
        def _():
            for part in range(len(parts)):
                copy(src, part, 0, sibling).wait_recv()

        @pl.when(near)
        def _():
            attend(src, False)

    @pl.loop(0, kv_local)
    def _(kv):
        for g in range(group):
            cols = slice(g * rows, (g + 1) * rows)
            head = acc[kv, :, cols] / lrow[kv, 0:1, cols]
            at = pl.ds(pl.multiple_of((kv * group + g) * HDIM, HDIM), HDIM)
            att_ref[:, at] = head.T.astype(jnp.bfloat16)

    w_copy.wait()
    chunks, _, width = psend.shape

    def exchange(n):
        return pltpu.make_async_remote_copy(
            src_ref=psend.at[n], dst_ref=precv.at[n],
            send_sem=ysend_sem.at[n], recv_sem=yrecv_sem.at[n],
            device_id={"hd": 1 - half}, device_id_type=MESH,
        )

    def project(first, n):
        at = pl.ds(pl.multiple_of((first * chunks + n) * width, width), width)
        return jnp.dot(att_ref[...], wbuf[:, at], preferred_element_type=jnp.float32)

    @pl.loop(0, chunks)
    def _(n):
        psend[n] = project(1 - half, n).astype(jnp.bfloat16)
        exchange(n).start()

    @pl.loop(0, chunks)
    def _(n):
        pown[n] = project(half, n)

    for n in range(chunks):
        exchange(n).wait_recv()
        proj_ref[:, n * width : (n + 1) * width] = (
            pown[n] + precv[n].astype(jnp.float32)
        ).astype(jnp.bfloat16)

    for n in range(chunks):
        exchange(n).wait_send()
    drain(me, always)

    @pl.loop(0, 4 * (levels + 1))
    def _(step):
        src, kind, held, _near = event(step)

        @pl.when(held & (lax.rem(kind, 2) == 0))
        def _():
            drain(src, kind == 0)


def fused_device(ctx_size, query_rows, key_rows, value_rows, doc_ids, out_weight):
    rows, q_cols = query_rows.shape
    kv_cols = key_rows.shape[1]
    kv_local = kv_cols // HDIM
    group = q_cols // kv_cols
    shard_blocks = rows // BLOCK
    reach = -(-(ctx_size * shard_blocks * 5 // 8 - 1) // shard_blocks)
    width = 256
    out_cols = out_weight.shape[1] // 2
    chunks = out_cols // width
    doc_tile = jnp.zeros((16, kv_cols), jnp.bfloat16).at[0:shard_blocks].set(
        jnp.broadcast_to(doc_ids.astype(jnp.bfloat16)[:, None], (shard_blocks, kv_cols))
    )
    vmem = pl.BlockSpec(memory_space=pltpu.VMEM)
    hbm = pl.BlockSpec(memory_space=pltpu.HBM)
    return pl.pallas_call(
        partial(fused_kernel, ctx_size // 4, reach),
        out_shape=(
            jax.ShapeDtypeStruct((rows, q_cols), jnp.bfloat16),
            jax.ShapeDtypeStruct((rows, out_cols), jnp.bfloat16),
        ),
        in_specs=[hbm, hbm, hbm, vmem, hbm],
        out_specs=(vmem, vmem),
        scratch_shapes=[
            pltpu.VMEM((rows, q_cols), jnp.bfloat16),
            pltpu.VMEM((ctx_size, 2 * rows + 16, kv_cols), jnp.bfloat16),
            pltpu.VMEM((kv_local, 2 * HDIM, group * rows), jnp.bfloat16),
            pltpu.VMEM((kv_local, HDIM, group * rows), jnp.float32),
            pltpu.VMEM((kv_local, 8, group * rows), jnp.float32),
            pltpu.VMEM((kv_local, 8, group * rows), jnp.float32),
            pltpu.VMEM(out_weight.shape, jnp.bfloat16),
            pltpu.VMEM((chunks, rows, width), jnp.bfloat16),
            pltpu.VMEM((chunks, rows, width), jnp.float32),
            pltpu.VMEM((chunks, rows, width), jnp.bfloat16),
            pltpu.SemaphoreType.DMA((3, ctx_size, 4)),
            pltpu.SemaphoreType.DMA((ctx_size, 4)),
            pltpu.SemaphoreType.DMA,
            pltpu.SemaphoreType.DMA((3,)),
            pltpu.SemaphoreType.DMA((chunks,)),
            pltpu.SemaphoreType.DMA((chunks,)),
        ],
        compiler_params=pltpu.CompilerParams(
            collective_id=0, has_side_effects=True, vmem_limit_bytes=44 * 1024 * 1024
        ),
    )(query_rows, key_rows, value_rows, doc_tile, out_weight)


def solution(mesh):
    in_specs = (P("ctx", "hd"), P("ctx", "hd"), P("ctx", "hd"), P("ctx"), P("hd", None))
    out_specs = (P("ctx", "hd"), P("ctx", "hd"))
    body = per_device
    if mesh.shape["ctx"] == 16 and mesh.shape["hd"] == 2:
        body = partial(fused_device, mesh.shape["ctx"])
    return jax.shard_map(
        body, mesh=mesh, in_specs=in_specs, out_specs=out_specs, check_vma=False
    )
```

```python
from functools import partial
import math

import jax
import jax.numpy as jnp
from jax import lax
from jax.experimental import pallas as pl
from jax.experimental.pallas import tpu as pltpu
from jax.sharding import PartitionSpec as P

HDIM = 128
BLOCK = 64


NEG_BIG = -1e30


def attend_part(
    softmax_state, shard_part, leading_row, query_heads, query_pos, query_doc, score_scale
):
    key_part, value_part, doc_part = shard_part
    row_count = key_part.shape[0]
    block_len = 256
    kv_local = query_heads.shape[1]
    key_blocks = key_part.reshape(row_count // block_len, block_len, kv_local, HDIM)
    value_blocks = value_part.reshape(row_count // block_len, block_len, kv_local, HDIM)
    doc_blocks = doc_part.reshape(row_count // block_len, block_len)

    def one_block(block_index, running):
        block_keys = key_blocks[block_index]
        block_values = value_blocks[block_index]
        key_pos = block_index * block_len + jnp.arange(block_len, dtype=jnp.int32)
        visible = (key_pos[None, :] <= query_pos[:, None]) & (key_pos[None, :] >= 0)
        visible = visible & (doc_blocks[block_index][None, :] == query_doc[:, None])

        def compute(inner_state):
            old_max, old_sum, old_weighted = inner_state
            scores = (
                jnp.einsum(
                    "tkgd,skd->kgts", query_heads, block_keys, preferred_element_type=jnp.float32
                )
                * score_scale
            )
            scores = jnp.where(visible[None, None], scores, NEG_BIG)
            new_max = jnp.maximum(old_max, jnp.max(scores, axis=-1))
            factor = jnp.exp(old_max - new_max)
            weights = jnp.where(visible[None, None], jnp.exp(scores - new_max[..., None]), 0.0)
            new_sum = old_sum * factor + jnp.sum(weights, axis=-1)
            update = jnp.einsum(
                "kgts,skd->kgtd",
                weights.astype(jnp.bfloat16),
                block_values,
                preferred_element_type=jnp.float32,
            )
            return (new_max, new_sum, old_weighted * factor[..., None] + update)

        return lax.cond(jnp.any(visible), compute, lambda inner_state: inner_state, running)

    return lax.fori_loop(0, row_count // block_len, one_block, softmax_state)


def attention_part(query_rows, key_rows, value_rows, doc_ids):
    tokens_here = query_rows.shape[0]
    kv_local = key_rows.shape[1] // HDIM
    group_size = query_rows.shape[1] // key_rows.shape[1]
    position = lax.axis_index("ctx")
    query_heads = query_rows.reshape(tokens_here, kv_local, group_size, HDIM)
    query_pos = position * tokens_here + jnp.arange(tokens_here, dtype=jnp.int32)
    token_docs = jnp.repeat(doc_ids, BLOCK)
    fold_part = partial(
        attend_part,
        query_heads=query_heads,
        query_pos=query_pos,
        query_doc=token_docs,
        score_scale=1.0 / math.sqrt(HDIM),
    )
    start_state = (
        jnp.full((kv_local, group_size, tokens_here), NEG_BIG, jnp.float32),
        jnp.zeros((kv_local, group_size, tokens_here), jnp.float32),
        jnp.zeros((kv_local, group_size, tokens_here, HDIM), jnp.float32),
    )
    softmax_state = fold_part(
        start_state,
        (
            lax.all_gather(key_rows, "ctx", axis=0, tiled=True),
            lax.all_gather(value_rows, "ctx", axis=0, tiled=True),
            lax.all_gather(token_docs, "ctx", axis=0, tiled=True),
        ),
        jnp.int32(0),
    )
    final_max, final_sum, final_weighted = softmax_state
    attended = final_weighted / final_sum[..., None]
    return (
        attended.transpose(2, 0, 1, 3)
        .reshape(tokens_here, kv_local * group_size * HDIM)
        .astype(jnp.bfloat16)
    )


def per_device(query_rows, key_rows, value_rows, doc_ids, out_weight):
    attended = attention_part(query_rows, key_rows, value_rows, doc_ids)
    partial_proj = jnp.dot(attended, out_weight, preferred_element_type=jnp.float32)
    projected = lax.psum_scatter(
        partial_proj.astype(jnp.bfloat16), "hd", scatter_dimension=1, tiled=True
    )
    return (attended, projected)

NEG_MASK = -1e30
LOG2E = 1.4426950408889634
MESH = pl.DeviceIdType.MESH


def fused_kernel(
    levels, reach, q_hbm, k_ref, v_ref, doc_ref, w_ref, att_ref, proj_ref,
    q_ref, buf, qa, acc, mrow, lrow, wbuf, psend, pown, precv,
    send_sem, recv_sem, w_sem, in_sem, ysend_sem, yrecv_sem,
):
    rows = q_ref.shape[0]
    kv_local = k_ref.shape[1] // HDIM
    group = q_ref.shape[1] // k_ref.shape[1]
    scale = LOG2E / math.sqrt(HDIM)
    v_at = rows + 16
    me = lax.axis_index("ctx")
    half = lax.axis_index("hd")
    z, x, c = lax.div(me, 4), lax.rem(lax.div(me, 2), 2), lax.rem(me, 2)
    up, across, sibling = me + 4, 4 * z + 2 * (1 - x) + c, 4 * z + 2 * x + (1 - c)
    across_chip = 4 * z + 2 * (1 - x)

    k_copy = pltpu.make_async_copy(k_ref, buf.at[me, pl.ds(0, rows)], in_sem.at[0])
    v_copy = pltpu.make_async_copy(v_ref, buf.at[me, pl.ds(v_at, rows)], in_sem.at[1])
    q_copy = pltpu.make_async_copy(q_hbm, q_ref, in_sem.at[2])
    k_copy.start()
    v_copy.start()
    q_copy.start()
    w_copy = pltpu.make_async_copy(w_ref, wbuf, w_sem)
    w_copy.start()

    barrier = pltpu.get_barrier_semaphore()
    pl.semaphore_signal(barrier, inc=1, device_id={"ctx": across}, device_id_type=MESH)
    pl.semaphore_signal(barrier, inc=1, device_id={"ctx": sibling}, device_id_type=MESH)
    pl.semaphore_signal(barrier, inc=1, device_id={"hd": 1 - half}, device_id_type=MESH)

    @pl.when(z + 1 < levels)
    def _():
        pl.semaphore_signal(barrier, inc=1, device_id={"ctx": up}, device_id_type=MESH)

    @pl.when(z > 0)
    def _():
        pl.semaphore_signal(barrier, inc=1, device_id={"ctx": me - 4}, device_id_type=MESH)

    buf[me, rows:v_at, :] = doc_ref[...]
    k_copy.wait()
    v_copy.wait()

    pl.semaphore_wait(
        barrier, 3 + jnp.where(z + 1 < levels, 1, 0) + jnp.where(z > 0, 1, 0)
    )

    middle = rows // 2
    parts = (
        (0, middle), (middle, v_at - middle), (v_at, middle), (v_at + middle, rows - middle)
    )

    def copy(src, part, direction, target):
        ref = buf.at[src, pl.ds(parts[part][0], parts[part][1])]
        return pltpu.make_async_remote_copy(
            src_ref=ref, dst_ref=ref,
            send_sem=send_sem.at[direction, src, part],
            recv_sem=recv_sem.at[src, part],
            device_id={"ctx": target}, device_id_type=MESH,
        )

    def sends(src, column, part):
        levels_down = z - lax.div(src, 4)
        by_column = column & (4 * (z + 1) - src <= reach)
        crossing = column & (src < across_chip) & (across_chip - src <= reach)
        if part >= 2:
            by_other = jnp.logical_not(column) & (levels_down == 2)
            by_column = (by_column | by_other) & (up - src <= reach)
            crossing = crossing & (levels_down < 3)
        return (
            (0, up, by_column & (z + 1 < levels)),
            (1, across, crossing),
            (2, sibling, (sibling > src) & (sibling - src <= reach)),
        )

    def forward(src, column, part):
        for direction, target, needed in sends(src, column, part):
            @pl.when(needed)
            def _():
                copy(src, part, direction, target).start()

    def drain(src, column):
        for part in range(len(parts)):
            for direction, target, needed in sends(src, column, part):
                @pl.when(needed)
                def _():
                    copy(src, part, direction, target).wait_send()

    always = me >= 0
    for part in range(len(parts)):
        forward(me, always, part)

    lane = lax.broadcasted_iota(jnp.int32, (1, rows), 1)
    docs = doc_ref[...].astype(jnp.float32)
    query_doc = jnp.zeros((1, rows), jnp.float32)
    for b in range(rows // BLOCK):
        inside = (lane >= b * BLOCK) & (lane < (b + 1) * BLOCK)
        query_doc = jnp.where(inside, docs[b : b + 1, 0:rows], query_doc)
    ids = lax.broadcasted_iota(jnp.int32, (HDIM, rows), 0).astype(jnp.float32)
    onehot = jnp.where(ids == query_doc, 1.0, 0.0).astype(jnp.bfloat16)
    q_copy.wait()
    for kv in range(kv_local):
        for g in range(group):
            head = (kv * group + g) * HDIM
            cols = slice(g * rows, (g + 1) * rows)
            qa[kv, 0:HDIM, cols] = q_ref[:, head : head + HDIM].T
            qa[kv, HDIM:, cols] = onehot

    def attend(src, diagonal):
        shard_docs = buf[src, rows:v_at, 0:HDIM].astype(jnp.float32)
        doc_lane = lax.broadcasted_iota(jnp.int32, (BLOCK, HDIM), 1).astype(jnp.float32)
        key_mask = jnp.concatenate(
            [
                jnp.where(doc_lane == shard_docs[b : b + 1, :], 0.0, NEG_MASK)
                for b in range(rows // BLOCK)
            ],
            axis=0,
        ).astype(jnp.bfloat16)

        heads = [(kv, g) for kv in range(kv_local) for g in range(group)]
        keys_of, values_of = {}, {}
        ones = jnp.ones((16, rows), jnp.bfloat16)

        def scores_of(kv, g):
            if kv not in keys_of:
                at = slice(kv * HDIM, (kv + 1) * HDIM)
                keys_of[kv] = jnp.concatenate([buf[src, 0:rows, at], key_mask], axis=1)
                values_of[kv] = jnp.concatenate([buf[src, v_at:, at].T, ones], axis=0)
            scores = jnp.dot(
                keys_of[kv],
                qa[kv, :, g * rows : (g + 1) * rows],
                preferred_element_type=jnp.float32,
            )
            if diagonal:
                key_pos = lax.broadcasted_iota(jnp.int32, scores.shape, 0)
                query_pos = lax.broadcasted_iota(jnp.int32, scores.shape, 1)
                scores = jnp.where(key_pos <= query_pos, scores, NEG_MASK)
            return scores

        ahead = 2
        ready = [scores_of(*head) for head in heads[:ahead]]
        for index, (kv, g) in enumerate(heads):
            cols = slice(g * rows, (g + 1) * rows)
            scores = ready.pop(0)
            if index + ahead < len(heads):
                ready.append(scores_of(*heads[index + ahead]))
            top = jnp.max(scores, axis=0, keepdims=True)
            if not diagonal:
                old = mrow[kv, 0:1, cols]
                top = jnp.maximum(top, old)
                factor = jnp.exp2((old - top) * scale)
            weights = jnp.exp2((scores - top) * scale)
            summed = jnp.dot(
                values_of[kv], weights.astype(jnp.bfloat16), preferred_element_type=jnp.float32
            )
            update, total = summed[0:HDIM], summed[HDIM : HDIM + 1]
            if not diagonal:
                total = total + lrow[kv, 0:1, cols] * factor
                update = update + acc[kv, :, cols] * factor
            mrow[kv, 0:1, cols] = top
            lrow[kv, 0:1, cols] = total
            acc[kv, :, cols] = update

    attend(me, True)

    def event(step):
        kind = lax.rem(step, 4)
        back = lax.div(step, 4) - jnp.where(kind >= 2, 1, 0)
        src_z = z - back
        src_x = jnp.where(kind >= 2, 1 - x, x)
        src_c = jnp.where(lax.rem(kind, 2) == 1, 1 - c, c)
        src = 4 * src_z + 2 * src_x + src_c
        near = (src < me) & (me - src <= reach)
        chip = 4 * z + 2 * x
        by_level = (kind == 0) & (back >= 1) & (4 * z - src <= reach)
        by_across = (kind == 2) & (src < chip) & (chip - src <= reach)
        by_sibling = (lax.rem(kind, 2) == 1) & near
        held = (back >= 0) & (src_z >= 0) & (by_level | by_across | by_sibling)
        return src, kind, held, held & near

    @pl.loop(0, 4 * (levels + 1))
    def _(step):
        src, kind, held, near = event(step)
        next_src, next_kind, next_held, next_near = event(step + 1)
        odd = lax.rem(kind, 2) == 1

        @pl.when(odd & next_held)
        def _():
            for part in range(len(parts)):
                @pl.when(next_near | (part < 2))
                def _():
                    copy(next_src, part, 0, sibling).wait_recv()
                    forward(next_src, next_kind == 0, part)

        @pl.when(odd & held)
        def _():
            for part in range(len(parts)):
                copy(src, part, 0, sibling).wait_recv()

        @pl.when(near)
        def _():
            attend(src, False)

    for kv in range(kv_local):
        for g in range(group):
            cols = slice(g * rows, (g + 1) * rows)
            head = acc[kv, :, cols] * (1.0 / lrow[kv, 0:1, cols])
            at = (kv * group + g) * HDIM
            att_ref[:, at : at + HDIM] = head.T.astype(jnp.bfloat16)

    w_copy.wait()
    chunks, _, width = psend.shape

    def exchange(n):
        return pltpu.make_async_remote_copy(
            src_ref=psend.at[n], dst_ref=precv.at[n],
            send_sem=ysend_sem.at[n], recv_sem=yrecv_sem.at[n],
            device_id={"hd": 1 - half}, device_id_type=MESH,
        )

    def project(first, n):
        at = pl.ds(pl.multiple_of((first * chunks + n) * width, width), width)
        return jnp.dot(att_ref[...], wbuf[:, at], preferred_element_type=jnp.float32)

    @pl.loop(0, chunks)
    def _(n):
        psend[n] = project(1 - half, n).astype(jnp.bfloat16)
        exchange(n).start()

    @pl.loop(0, chunks)
    def _(n):
        pown[n] = project(half, n)

    for n in range(chunks):
        exchange(n).wait_recv()
        proj_ref[:, n * width : (n + 1) * width] = (
            pown[n] + precv[n].astype(jnp.float32)
        ).astype(jnp.bfloat16)

    for n in range(chunks):
        exchange(n).wait_send()
    drain(me, always)

    @pl.loop(0, 4 * (levels + 1))
    def _(step):
        src, kind, held, _near = event(step)

        @pl.when(held & (lax.rem(kind, 2) == 0))
        def _():
            drain(src, kind == 0)


def fused_device(ctx_size, query_rows, key_rows, value_rows, doc_ids, out_weight):
    rows, q_cols = query_rows.shape
    kv_cols = key_rows.shape[1]
    kv_local = kv_cols // HDIM
    group = q_cols // kv_cols
    shard_blocks = rows // BLOCK
    reach = -(-(ctx_size * shard_blocks * 5 // 8 - 1) // shard_blocks)
    width = 256
    out_cols = out_weight.shape[1] // 2
    chunks = out_cols // width
    doc_tile = jnp.zeros((16, kv_cols), jnp.bfloat16).at[0:shard_blocks].set(
        jnp.broadcast_to(doc_ids.astype(jnp.bfloat16)[:, None], (shard_blocks, kv_cols))
    )
    vmem = pl.BlockSpec(memory_space=pltpu.VMEM)
    hbm = pl.BlockSpec(memory_space=pltpu.HBM)
    return pl.pallas_call(
        partial(fused_kernel, ctx_size // 4, reach),
        out_shape=(
            jax.ShapeDtypeStruct((rows, q_cols), jnp.bfloat16),
            jax.ShapeDtypeStruct((rows, out_cols), jnp.bfloat16),
        ),
        in_specs=[hbm, hbm, hbm, vmem, hbm],
        out_specs=(vmem, vmem),
        scratch_shapes=[
            pltpu.VMEM((rows, q_cols), jnp.bfloat16),
            pltpu.VMEM((ctx_size, 2 * rows + 16, kv_cols), jnp.bfloat16),
            pltpu.VMEM((kv_local, 2 * HDIM, group * rows), jnp.bfloat16),
            pltpu.VMEM((kv_local, HDIM, group * rows), jnp.float32),
            pltpu.VMEM((kv_local, 8, group * rows), jnp.float32),
            pltpu.VMEM((kv_local, 8, group * rows), jnp.float32),
            pltpu.VMEM(out_weight.shape, jnp.bfloat16),
            pltpu.VMEM((chunks, rows, width), jnp.bfloat16),
            pltpu.VMEM((chunks, rows, width), jnp.float32),
            pltpu.VMEM((chunks, rows, width), jnp.bfloat16),
            pltpu.SemaphoreType.DMA((3, ctx_size, 4)),
            pltpu.SemaphoreType.DMA((ctx_size, 4)),
            pltpu.SemaphoreType.DMA,
            pltpu.SemaphoreType.DMA((3,)),
            pltpu.SemaphoreType.DMA((chunks,)),
            pltpu.SemaphoreType.DMA((chunks,)),
        ],
        compiler_params=pltpu.CompilerParams(
            collective_id=0, has_side_effects=True, vmem_limit_bytes=44 * 1024 * 1024
        ),
    )(query_rows, key_rows, value_rows, doc_tile, out_weight)


def solution(mesh):
    in_specs = (P("ctx", "hd"), P("ctx", "hd"), P("ctx", "hd"), P("ctx"), P("hd", None))
    out_specs = (P("ctx", "hd"), P("ctx", "hd"))
    body = per_device
    if mesh.shape["ctx"] == 16 and mesh.shape["hd"] == 2:
        body = partial(fused_device, mesh.shape["ctx"])
    return jax.shard_map(
        body, mesh=mesh, in_specs=in_specs, out_specs=out_specs, check_vma=False
    )
```
